32 devices in a mesh: member: 8 (over z, y), tile: 4 (over x, core).
Axes of the slice: x: 2, y: 2, z: 4, core: 2. Of those that a mesh axis runs over, the one named last changes fastest.
Arguments:
- features: bfloat16 [8, 128, 32, 2048], P('member', None, 'tile')
- residual_state: float32 [8, 4, 32, 2048], P('member', None, 'tile'), may hold values from -6 to 6
- noise: float32 [8, 4, 32, 2048], P('member', None, 'tile'), may hold values from -6 to 6
- regression_mean: float32 [4, 32, 2048], P(None, 'tile', 'member'), may hold values from -6 to 6
- step_index: int32 [1], replicated, may hold values from 9 to 16
- conv_first: bfloat16 [9, 128, 128], replicated, may hold values from -0.1875 to 0.1875
- conv_second: bfloat16 [9, 128, 128], replicated, may hold values from -0.1875 to 0.1875
- head_weight: bfloat16 [4, 128], replicated, may hold values from -0.5 to 0.5
- spread_target: float32 [4], replicated, may hold values from 0.5 to 4
Outputs:
- ensemble_field: float32 [8, 4, 32, 2048], P('member', None, 'tile')
- next_state: float32 [8, 4, 32, 2048], P('member', None, 'tile')
The draws below stay inside these ranges and needn't reach their ends.
All inputs are finite; a program needn't handle non-finite values.
Results may differ from the reference program's by a relative error of at most 0.0013.
Values may be sent and summed in bfloat16 or wider, within the bound.
A program may use at most 128 MiB of HBM per device.

```python
import math
import jax
import jax.numpy as jnp
from jax import lax

CHANNELS = 128
GROUPS = 32
OUTPUTS = 4
COLS = 2048
ROWS = 32
MEMBERS = 8


def draw_features(key, part):
    key = jax.random.fold_in(key, 7)
    key_values, key_rows, key_cols = jax.random.split(key, 3)
    shape = (MEMBERS, CHANNELS, ROWS, COLS)
    position = jnp.arange(ROWS).astype(jnp.float32) / max(ROWS - 1, 1)
    ramp = jnp.exp(position * math.log(3.0))
    row_scale = ramp * jnp.exp(jax.random.uniform(key_rows, (ROWS,), jnp.float32, 0.0, math.log(3.3)))
    col_scale = jnp.exp(jax.random.uniform(key_cols, (COLS,), jnp.float32, 0.0, math.log(3.3)))
    scale = row_scale[:, None] * col_scale[None, :] / 6.0
    values = jax.random.normal(key_values, shape, jnp.float32)
    return (values * scale[None, None]).astype(jnp.bfloat16)


def level_of(rng, extent, cuts, low, top_value):
    factor_of = 1.0
    for dim, blocks in cuts:
        steps = jax.random.uniform(jax.random.fold_in(jax.random.fold_in(rng, 6), dim), (blocks,), jnp.float32, low / len(cuts), top_value / len(cuts))
        factor_of = factor_of * jnp.repeat(jnp.exp(steps), extent[dim] // blocks).reshape((-1,) + (1,) * (len(extent) - 1 - dim))
    return factor_of


def normal_values(own_key, shape, scale, bound, cuts=(), held_as=jnp.bfloat16):
    result = jax.random.normal(own_key, shape, jnp.float32) * scale
    if len(cuts) > 0:
        result = level_of(own_key, shape, cuts, -0.22, 0.18) * result
    return jnp.clip(result, min=-bound, max=bound).astype(held_as)


def setup_inputs(seed: int = 0) -> dict:
    arg_keys = jax.random.split(jax.random.key(seed), 10)
    return {
        "features": draw_features(jax.random.fold_in(arg_keys[9], 71), 0),
        "residual_state": normal_values(arg_keys[1], (MEMBERS, OUTPUTS, ROWS, COLS), 1.0, 6.0, ((0, 8), (2, 4)), jnp.float32),
        "noise": normal_values(arg_keys[2], (MEMBERS, OUTPUTS, ROWS, COLS), 1.0, 6.0, ((0, 8), (2, 4)), jnp.float32),
        "regression_mean": normal_values(arg_keys[3], (OUTPUTS, ROWS, COLS), 1.0, 6.0, ((1, 4), (2, 8)), jnp.float32),
        "step_index": jax.random.randint(arg_keys[4], (1,), 9, 17).astype(jnp.int32),
        "conv_first": normal_values(arg_keys[5], (9, CHANNELS, CHANNELS), (9 * CHANNELS) ** -0.5, 0.1875),
        "conv_second": normal_values(arg_keys[6], (9, CHANNELS, CHANNELS), (9 * CHANNELS) ** -0.5, 0.1875),
        "head_weight": normal_values(arg_keys[7], (OUTPUTS, CHANNELS), CHANNELS ** -0.5, 0.5),
        "spread_target": jnp.clip(jnp.exp(jax.random.uniform(arg_keys[8], (OUTPUTS,), jnp.float32, math.log(0.5), math.log(4.0))), 0.5, 4.0),
    }


def plan(step_index):
    steps = jnp.arange(18).astype(jnp.float32)
    upper = 800.0 ** (1.0 / 7.0)
    lower = 0.002 ** (1.0 / 7.0)
    sigmas = (upper + steps / 17.0 * (lower - upper)) ** 7
    places = jnp.arange(18).astype(jnp.int32)
    sigma = jnp.sum(jnp.where(places == step_index[0], sigmas, 0.0))
    sigma_next = jnp.sum(jnp.where(places == step_index[0] + 1, sigmas, 0.0))
    return (sigma, sigma_next)

def group_norm(block):
    values = block.astype(jnp.float32).reshape(GROUPS, -1, block.shape[1], block.shape[2])
    mean = lax.optimization_barrier(jnp.mean(values, axis=(1, 2, 3), keepdims=True))
    centred = values - mean
    var = lax.optimization_barrier(jnp.mean(centred * centred, axis=(1, 2, 3), keepdims=True))
    normed = centred * lax.rsqrt(var + 1e-05)
    return jax.nn.silu(normed).astype(jnp.bfloat16).reshape(block.shape)

def convolve(activ, kernel):
    height, width = (activ.shape[1], activ.shape[2])
    padded = jnp.pad(activ.astype(jnp.float32), ((0, 0), (1, 1), (1, 1)))
    total = jnp.zeros((kernel.shape[1], height, width), jnp.float32)
    for row_tap in range(3):
        for col_tap in range(3):
            weight = kernel[3 * row_tap + col_tap].astype(jnp.float32)
            window = padded[:, row_tap:row_tap + height, col_tap:col_tap + width]
            total = total + jnp.einsum('oc,chw->ohw', weight, window)
    return total

def reference(features, residual_state, noise, regression_mean, step_index, conv_first, conv_second, head_weight, spread_target):
    sigma, sigma_next = plan(step_index)
    sigma_hat = 1.25 * sigma

    def network_of(member_features):
        activ_first = group_norm(member_features)
        hidden_first = convolve(activ_first, conv_first).astype(jnp.bfloat16)
        activ_second = group_norm(hidden_first)
        block_out = (member_features.astype(jnp.float32) + convolve(activ_second, conv_second)).astype(jnp.bfloat16)
        return jnp.einsum('oc,chw->ohw', head_weight.astype(jnp.float32), block_out.astype(jnp.float32))
    network = lax.map(network_of, features)
    state_hat = residual_state + jnp.sqrt(sigma_hat * sigma_hat - sigma * sigma) * noise
    c_skip = 0.25 / (sigma_hat * sigma_hat + 0.25)
    c_out = 0.5 * sigma_hat / jnp.sqrt(sigma_hat * sigma_hat + 0.25)
    denoised = c_skip * state_hat + c_out * network
    next_state = state_hat + (sigma_next - sigma_hat) / sigma_hat * (state_hat - denoised)
    ens_mean = lax.optimization_barrier(jnp.mean(next_state, axis=0))
    ens_var = lax.optimization_barrier(jnp.mean(next_state * next_state, axis=0)) - ens_mean * ens_mean
    factor = jnp.sqrt(1.0 + spread_target[:, None, None] / (ens_var + 1.0))
    ensemble_field = regression_mean[None] + ens_mean[None] + (next_state - ens_mean[None]) * factor[None]
    return (ensemble_field, next_state)
```

```python
import functools

import jax
import jax.numpy as jnp
from jax import lax
from jax.experimental import pallas as pl
from jax.experimental.pallas import tpu as pltpu
from jax.sharding import PartitionSpec as P

GROUPS = 32
EPS = 1e-05
F32 = jnp.float32
BF16 = jnp.bfloat16
MESH = pl.DeviceIdType.MESH


def lane_to_row(column):
    n = column.shape[0]
    same = lax.broadcasted_iota(jnp.int32, (n, n), 0) == lax.broadcasted_iota(jnp.int32, (n, n), 1)
    return jnp.sum(jnp.where(same, column, 0.0), axis=0, keepdims=True)


def kernel(tiles, members, fused, chans, rows, cols, step, *refs):
    if fused:
        (coef, target, feat, resid, noise, regr, wa, wb, head, out_next, out_field) = refs[:11]
        refs = refs[11:]
    else:
        (coef, target, feat, resid, noise, wa, wb, head, out_next) = refs[:9]
        refs = refs[9:]
    (fbuf, xt, hid, act, wide, hw, perm, pivot, acc1, acc2, meanb, rstdb, stat,
     fsem, ssem, rsem, hs, hr) = refs[:18]
    if fused:
        ens_in, back_out, back_in, es, er, bs, br = refs[18:]
    me_t = lax.axis_index("tile")
    me_m = lax.axis_index("member")
    top = me_t > 0
    bottom = me_t < tiles - 1
    chunks = cols // step
    per = 256 // rows
    parts = chans // per
    pairs = rows // 2

    for k in range(parts):
        pltpu.make_async_copy(
            feat.at[pl.ds(k * 256, 256)], fbuf.at[pl.ds(k * 256, 256)], fsem.at[k]
        ).start()

    barrier = pltpu.get_barrier_semaphore()
    for d in range(1, tiles):
        pl.semaphore_signal(barrier, inc=1, device_id={"tile": lax.rem(me_t + d, tiles)}, device_id_type=MESH)
    greet = tiles - 1
    if fused:
        for d in range(1, members):
            pl.semaphore_signal(
                barrier, inc=1, device_id={"member": lax.rem(me_m + d, members)}, device_id_type=MESH
            )
        greet += members - 1

    wide[...] = jnp.zeros_like(wide)
    for which, source in enumerate((wa, wb)):
        for out_row in range(2):
            for tap_row in range(3):
                for tap_col in range(3):
                    at = (out_row + tap_row) * 3 * chans + tap_col * chans
                    wide[which, out_row * chans : (out_row + 1) * chans, at : at + chans] = source[
                        3 * tap_row + tap_col
                    ]
    hw[...] = jnp.zeros_like(hw)
    outs = head.shape[0]
    head32 = head[...].astype(F32)
    for p in range(pairs):
        for out_row in range(2):
            place = lax.broadcasted_iota(jnp.int32, (rows, chans), 0) == 2 * p + out_row
            for o in range(outs):
                hw[p, o * rows : (o + 1) * rows, out_row * chans : (out_row + 1) * chans] = jnp.where(
                    place, head32[o : o + 1, :], 0.0
                ).astype(BF16)
    to = lax.broadcasted_iota(jnp.int32, (256, 256), 0)
    frm = lax.broadcasted_iota(jnp.int32, (256, 256), 1)
    perm[...] = jnp.where((to // per == frm % rows) & (to % per == frm // rows), 1.0, 0.0).astype(BF16)
    acc1[...] = jnp.zeros_like(acc1)
    acc2[...] = jnp.zeros_like(acc2)

    def fold(values):
        total = values[:, :128]
        for at in range(128, values.shape[1], 128):
            total = total + values[:, at : at + 128]
        return total

    def accumulate(start, blocks, first):
        size = blocks[0].shape[0]
        where = pl.ds(start, size)

        @pl.when(first)
        def _():
            pivot[where, :] = jnp.broadcast_to(
                jnp.mean(blocks[0][:, :128], axis=1, keepdims=True), (size, 128)
            )

        base = pivot[where, :]
        one = jnp.zeros((size, 128), F32)
        two = jnp.zeros((size, 128), F32)
        for block in blocks:
            for at in range(0, block.shape[1], 128):
                off = block[:, at : at + 128] - base
                one = one + off
                two = two + off * off
        acc1[where, :] += one
        acc2[where, :] += two

    for k in range(parts):
        pltpu.make_async_copy(
            feat.at[pl.ds(k * 256, 256)], fbuf.at[pl.ds(k * 256, 256)], fsem.at[k]
        ).wait()

        def spread(j, carry, k=k):
            at = pl.ds(pl.multiple_of(j * step, step), step)
            moved = jnp.dot(perm[...], fbuf[k * 256 : (k + 1) * 256, at], preferred_element_type=F32)
            blocks = [moved[r * per : (r + 1) * per] for r in range(rows)]
            for r in range(rows):
                start = (1 + r) * chans + k * per
                xt[start : start + per, at] = blocks[r].astype(BF16)
            accumulate(k * per, blocks, j == 0)
            return carry

        lax.fori_loop(0, chunks, spread, 0)

    pl.semaphore_wait(barrier, greet)

    def halo(buf, turn, side):
        mine, theirs = ((1, rows + 1), (rows, 0))[side]
        return pltpu.make_async_remote_copy(
            src_ref=buf.at[pl.ds(mine * chans, chans)],
            dst_ref=buf.at[pl.ds(theirs * chans, chans)],
            send_sem=hs.at[turn, side],
            recv_sem=hr.at[turn, side],
            device_id={"tile": me_t - 1 if side == 0 else me_t + 1},
            device_id_type=MESH,
        )

    def send_halo(buf, turn, side):
        @pl.when(top if side == 0 else bottom)
        def _():
            halo(buf, turn, side).start()

    def stat_copy(turn, src, dev, d):
        return pltpu.make_async_remote_copy(
            src_ref=stat.at[turn, src],
            dst_ref=stat.at[turn, src],
            send_sem=ssem.at[turn, d],
            recv_sem=rsem.at[turn, src],
            device_id={"tile": dev},
            device_id_type=MESH,
        )

    count = rows * cols

    def norm_values(turn):
        one = jnp.sum(acc1[...], axis=1, keepdims=True)
        two = jnp.sum(acc2[...], axis=1, keepdims=True)
        mean = pivot[:, 0:1] + one / count
        dev2 = jnp.maximum(two - one * one / count, 0.0)
        row_id = lax.broadcasted_iota(jnp.int32, (8, chans), 0)
        stat[turn, me_t] = jnp.where(row_id == 0, lane_to_row(mean), lane_to_row(dev2))
        for d in range(1, tiles):
            stat_copy(turn, me_t, lax.rem(me_t + d, tiles), d).start()
        for d in range(1, tiles):
            other = lax.rem(me_t + d, tiles)
            stat_copy(turn, other, other, d).wait_recv()
        size = chans // GROUPS
        group = (
            lax.broadcasted_iota(jnp.int32, (chans, chans), 0) // size
            == lax.broadcasted_iota(jnp.int32, (chans, chans), 1) // size
        )
        every = [stat[turn, t] for t in range(tiles)]
        total = sum(one_of[0:1, :] for one_of in every)
        gmean = jnp.sum(jnp.where(group, total, 0.0), axis=1, keepdims=True) / (size * tiles)
        dev = jnp.zeros((chans, chans), F32)
        for one_of in every:
            gap = one_of[0:1, :] - gmean
            dev = dev + (one_of[1:2, :] + count * (gap * gap))
        gvar = jnp.sum(jnp.where(group, dev, 0.0), axis=1, keepdims=True) / (size * tiles * count)
        meanb[...] = jnp.broadcast_to(gmean, meanb.shape)
        rstdb[...] = jnp.broadcast_to(0.5 * lax.rsqrt(gvar + EPS), rstdb.shape)
        for d in range(1, tiles):
            stat_copy(turn, me_t, lax.rem(me_t + d, tiles), d).wait_send()

    lane = lax.broadcasted_iota(jnp.int32, (16, cols), 1)

    def activate(src, first_row, n_rows):
        def body(i, carry):
            row = first_row + i // (chans // 16)
            block = (i % (chans // 16)) * 16
            here = pl.ds(pl.multiple_of(block, 16), 16)
            value = src[pl.ds(pl.multiple_of(row * chans + block, 16), 16), :].astype(F32)
            half = (value - meanb[here, 0:1]) * rstdb[here, 0:1]
            result = half + half * jnp.tanh(half)
            before = jnp.where(lane == 0, 0.0, pltpu.roll(result, 1, 1))
            after = jnp.where(lane == cols - 1, 0.0, pltpu.roll(result, cols - 1, 1))
            for tap, one_of in enumerate((before, result, after)):
                start = pl.multiple_of(row * 3 * chans + tap * chans + block, 16)
                act[pl.ds(start, 16), :] = one_of.astype(BF16)
            return carry

        lax.fori_loop(0, n_rows * (chans // 16), body, 0)

    def activate_all(buf, turn):
        activate(buf, 1, rows)
        for side, row in ((0, rows + 1), (1, 0)):
            there = bottom if side == 0 else top

            @pl.when(there)
            def _(side=side, row=row):
                halo(buf, turn, side).wait_recv()
                activate(buf, row, 1)

            @pl.when(jnp.logical_not(there))
            def _(row=row):
                act[row * 3 * chans : (row + 1) * 3 * chans, :] = jnp.zeros((3 * chans, cols), BF16)

    def finish_halo(buf, turn):
        for side, there in ((0, top), (1, bottom)):
            @pl.when(there)
            def _(side=side):
                halo(buf, turn, side).wait_send()

    def conv(which, p, at):
        start = p * 6 * chans
        if not isinstance(p, int):
            start = pl.multiple_of(start, 128)
        return jnp.dot(wide[which], act[pl.ds(start, 12 * chans), at], preferred_element_type=F32)

    send_halo(xt, 0, 0)
    send_halo(xt, 0, 1)
    norm_values(0)
    activate_all(xt, 0)
    acc1[...] = jnp.zeros_like(acc1)
    acc2[...] = jnp.zeros_like(acc2)

    def first_conv(i, carry):
        p = lax.rem(3 * i, pairs)

        def over_cols(j, inner):
            at = pl.ds(pl.multiple_of(j * step, step), step)
            result = conv(0, p, at).astype(BF16)
            hid[pl.ds(pl.multiple_of((1 + 2 * p) * chans, chans), 2 * chans), at] = result
            wide_result = result.astype(F32)
            accumulate(0, [wide_result[:chans], wide_result[chans:]], (i == 0) & (j == 0))
            return inner

        lax.fori_loop(0, chunks, over_cols, 0)

        @pl.when(i == 0)
        def _():
            send_halo(hid, 1, 0)

        @pl.when(i == 1)
        def _():
            send_halo(hid, 1, 1)

        return carry

    lax.fori_loop(0, pairs, first_conv, 0)
    norm_values(1)
    activate_all(hid, 1)

    at_step = jnp.full((8, 128), coef[0], jnp.int32).astype(F32)
    upper = 800.0 ** (1.0 / 7.0)
    lower = 0.002 ** (1.0 / 7.0)

    def level(place):
        base = upper + place / 17.0 * (lower - upper)
        square = base * base
        return base * square * (square * square)

    sigma = level(at_step)
    sigma_next = level(at_step + 1.0)
    sigma_hat = 1.25 * sigma
    spread_of = jnp.sqrt(sigma_hat * sigma_hat - sigma * sigma)[0:1, 0:1]
    c_skip = (0.25 / (sigma_hat * sigma_hat + 0.25))[0:1, 0:1]
    c_out = (0.5 * sigma_hat / jnp.sqrt(sigma_hat * sigma_hat + 0.25))[0:1, 0:1]
    drift = ((sigma_next - sigma_hat) / sigma_hat)[0:1, 0:1]

    def advance(j):
        at = pl.ds(pl.multiple_of(j * step, step), step)
        network = jnp.zeros((outs * rows, step), F32)
        for p in range(pairs):
            start = (1 + 2 * p) * chans
            block = (xt[start : start + 2 * chans, at].astype(F32) + conv(1, p, at)).astype(BF16)
            network = network + jnp.dot(hw[p], block, preferred_element_type=F32)
        state_hat = resid[:, at] + spread_of * noise[:, at]
        denoised = c_skip * state_hat + c_out * network
        out_next[:, at] = state_hat + drift * (state_hat - denoised)

    if not fused:
        lax.fori_loop(0, chunks, lambda j, c: (advance(j), c)[1], 0)
        finish_halo(xt, 0)
        finish_halo(hid, 1)
        return

    width = cols // members
    ratio = width // step

    def state_copy(owner, sender):
        return pltpu.make_async_remote_copy(
            src_ref=out_next.at[:, pl.ds(pl.multiple_of(owner * width, width), width)],
            dst_ref=ens_in.at[sender],
            send_sem=es.at[owner],
            recv_sem=er.at[sender],
            device_id={"member": owner},
            device_id_type=MESH,
        )

    def back_copy(owner, member):
        return pltpu.make_async_remote_copy(
            src_ref=back_out,
            dst_ref=back_in.at[owner],
            send_sem=bs.at[member],
            recv_sem=br.at[owner],
            device_id={"member": member},
            device_id_type=MESH,
        )

    def ensemble():
        for d in range(1, members):
            other = lax.rem(me_m + d, members)
            state_copy(me_m, other).wait_recv()
        for o in range(outs):
            sub = pl.ds(o * rows, rows)
            one = jnp.zeros((rows, width), F32)
            two = jnp.zeros((rows, width), F32)
            for m in range(members):
                value = ens_in[m, sub, :]
                one = one + value
                two = two + value * value
            mean = one / members
            var = two / members - mean * mean
            factor = jnp.sqrt(1.0 + target[o] / (var + 1.0))
            back_out[0, sub, :] = regr[sub, :] + (mean - mean * factor)
            back_out[1, sub, :] = factor
        for d in range(1, members):
            back_copy(me_m, lax.rem(me_m + d, members)).start()
        mine = pl.ds(pl.multiple_of(me_m * width, width), width)
        out_field[:, mine] = back_out[0] + out_next[:, mine] * back_out[1]

    def turn_of(owner, carry):
        @pl.when(owner < members)
        def _():
            for part in range(ratio):
                advance(owner * ratio + part)

            @pl.when(owner != me_m)
            def _():
                state_copy(owner, me_m).start()

            @pl.when(owner == me_m)
            def _():
                ens_in[me_m] = out_next[:, pl.ds(pl.multiple_of(owner * width, width), width)]

        @pl.when(owner == me_m + 1)
        def _():
            ensemble()

        return carry

    lax.fori_loop(0, members + 1, turn_of, 0)

    def collect(d, carry):
        owner = lax.rem(me_m + d, members)
        back_copy(owner, owner).wait_recv()
        at = pl.ds(pl.multiple_of(owner * width, width), width)
        out_field[:, at] = back_in[owner, 0] + out_next[:, at] * back_in[owner, 1]
        return carry

    lax.fori_loop(1, members, collect, 0)
    for d in range(1, members):
        other = lax.rem(me_m + d, members)
        state_copy(other, me_m).wait_send()
        back_copy(me_m, other).wait_send()
    finish_halo(xt, 0)
    finish_halo(hid, 1)


def shards(
    features,
    residual_state,
    noise,
    regression_mean,
    step_index,
    conv_first,
    conv_second,
    head_weight,
    spread_target,
):
    tiles = lax.axis_size("tile")
    members = lax.axis_size("member")
    _, chans, rows, cols = features.shape
    outs = residual_state.shape[1]
    step = 256
    fused = (cols // members) % step == 0
    flat = outs * rows
    padded = rows + 2
    vmem = pl.BlockSpec(memory_space=pltpu.VMEM)
    smem = pl.BlockSpec(memory_space=pltpu.SMEM)
    operands = [
        (smem, step_index),
        (smem, spread_target),
        (pl.BlockSpec(memory_space=pl.ANY), features.reshape(chans * rows, cols)),
        (vmem, residual_state.reshape(flat, cols)),
        (vmem, noise.reshape(flat, cols)),
        (vmem, regression_mean.reshape(flat, cols // members)),
        (vmem, conv_first),
        (vmem, conv_second),
        (vmem, head_weight),
    ]
    if not fused:
        del operands[5]
    dma = pltpu.SemaphoreType.DMA
    scratch = [
        pltpu.VMEM((chans * rows, cols), BF16),
        pltpu.VMEM((padded * chans, cols), BF16),
        pltpu.VMEM((padded * chans, cols), BF16),
        pltpu.VMEM((padded * 3 * chans, cols), BF16),
        pltpu.VMEM((2, 2 * chans, 12 * chans), BF16),
        pltpu.VMEM((rows // 2, flat, 2 * chans), BF16),
        pltpu.VMEM((256, 256), BF16),
        pltpu.VMEM((chans, 128), F32),
        pltpu.VMEM((chans, 128), F32),
        pltpu.VMEM((chans, 128), F32),
        pltpu.VMEM((chans, 128), F32),
        pltpu.VMEM((chans, 128), F32),
        pltpu.VMEM((2, tiles, 8, chans), F32),
        dma((chans * rows // 256,)),
        dma((2, tiles)),
        dma((2, tiles)),
        dma((2, 2)),
        dma((2, 2)),
    ]
    if fused:
        scratch += [
            pltpu.VMEM((members, flat, cols // members), F32),
            pltpu.VMEM((2, flat, cols // members), F32),
            pltpu.VMEM((members, 2, flat, cols // members), F32),
            dma((members,)),
            dma((members,)),
            dma((members,)),
            dma((members,)),
        ]
    result = pl.pallas_call(
        functools.partial(kernel, tiles, members, fused, chans, rows, cols, step),
        out_shape=[jax.ShapeDtypeStruct((flat, cols), F32)] * (2 if fused else 1),
        in_specs=[spec for spec, _ in operands],
        out_specs=[vmem] * (2 if fused else 1),
        scratch_shapes=scratch,
        compiler_params=pltpu.CompilerParams(
            collective_id=0, has_side_effects=True, vmem_limit_bytes=52 * 1024 * 1024
        ),
    )(*[value for _, value in operands])
    advanced = result[0].reshape(outs, rows, cols)
    if fused:
        return (result[1].reshape(1, outs, rows, cols), advanced[None])
    target = spread_target[:, None, None]
    regional = lax.all_gather(regression_mean, "member", axis=2, tiled=True)
    first, second = lax.psum((advanced, advanced * advanced), "member")
    ens_mean = first / members
    ens_var = second / members - ens_mean * ens_mean
    factor = jnp.sqrt(1.0 + target / (ens_var + 1.0))
    field = regional + ens_mean + (advanced - ens_mean) * factor
    return (field[None], advanced[None])


def solution(mesh):
    return jax.shard_map(
        shards,
        mesh=mesh,
        in_specs=(
            P("member", None, "tile", None),
            P("member", None, "tile", None),
            P("member", None, "tile", None),
            P(None, "tile", "member"),
            P(),
            P(),
            P(),
            P(),
            P(),
        ),
        out_specs=(P("member", None, "tile", None), P("member", None, "tile", None)),
        check_vma=False,
    )
```

```python
import functools

import jax
import jax.numpy as jnp
from jax import lax
from jax.experimental import pallas as pl
from jax.experimental.pallas import tpu as pltpu
from jax.sharding import PartitionSpec as P

GROUPS = 32
EPS = 1e-05
F32 = jnp.float32
BF16 = jnp.bfloat16
MESH = pl.DeviceIdType.MESH


def log2(n):
    assert n & (n - 1) == 0
    return n.bit_length() - 1


def lane_to_row(column):
    n = column.shape[0]
    same = lax.broadcasted_iota(jnp.int32, (n, n), 0) == lax.broadcasted_iota(jnp.int32, (n, n), 1)
    return jnp.sum(jnp.where(same, column, 0.0), axis=0, keepdims=True)


def kernel(tiles, members, fused, chans, rows, cols, step, *refs):
    if fused:
        (coef, target, feat, resid_h, noise_h, regr_h, wa_h, wb_h, head, out_next, out_field) = refs[:11]
        refs = refs[11:]
    else:
        (coef, target, feat, resid_h, noise_h, wa_h, wb_h, head, out_next) = refs[:9]
        refs = refs[9:]
    acts = refs[: rows // 2 + 1]
    refs = refs[rows // 2 + 1 :]
    (fbuf, xt, hid, wide, hw, perm, pivot, acc1, acc2, meanb, rstdb, stat, resid, noise, wa, wb,
     fsem, ssem, rsem, hs, hr, osem) = refs[:22]
    if fused:
        ens_in, back_out, back_in, regr, es, er, bs, br = refs[22:]
    me_t = lax.axis_index("tile")
    me_m = lax.axis_index("member")
    top = me_t > 0
    bottom = me_t < tiles - 1
    chunks = cols // step
    per = 256 // rows
    parts = chans // per
    pairs = rows // 2

    for k in range(parts):
        pltpu.make_async_copy(
            feat.at[pl.ds(k * 256, 256)], fbuf.at[pl.ds(k * 256, 256)], fsem.at[k]
        ).start()
    pairs_of = [(wa_h, wa), (wb_h, wb), (resid_h, resid), (noise_h, noise)]
    if fused:
        pairs_of.append((regr_h, regr))
    loads = [pltpu.make_async_copy(a, b, osem.at[n]) for n, (a, b) in enumerate(pairs_of)]
    for load in loads:
        load.start()

    barrier = pltpu.get_barrier_semaphore()
    for d in range(1, tiles):
        pl.semaphore_signal(barrier, inc=1, device_id={"tile": lax.rem(me_t + d, tiles)}, device_id_type=MESH)
    greet = tiles - 1
    if fused:
        for d in range(1, members):
            pl.semaphore_signal(
                barrier, inc=1, device_id={"member": lax.rem(me_m + d, members)}, device_id_type=MESH
            )
        greet += members - 1

    hw[...] = jnp.zeros_like(hw)
    outs = head.shape[0]
    head32 = head[...].astype(F32)
    for p in range(pairs):
        for out_row in range(2):
            place = lax.broadcasted_iota(jnp.int32, (rows, chans), 0) == 2 * p + out_row
            for o in range(outs):
                hw[p, o * rows : (o + 1) * rows, out_row * chans : (out_row + 1) * chans] = jnp.where(
                    place, head32[o : o + 1, :], 0.0
                ).astype(BF16)
    to = lax.broadcasted_iota(jnp.int32, (256, 256), 0)
    frm = lax.broadcasted_iota(jnp.int32, (256, 256), 1)
    perm[...] = jnp.where((to & (per - 1)) * rows + (to >> log2(per)) == frm, 1.0, 0.0).astype(BF16)
    acc1[...] = jnp.zeros_like(acc1)
    acc2[...] = jnp.zeros_like(acc2)

    def fold(values):
        total = values[:, :128]
        for at in range(128, values.shape[1], 128):
            total = total + values[:, at : at + 128]
        return total

    def accumulate(start, blocks, first):
        size = blocks[0].shape[0]
        where = pl.ds(start, size)

        def _():
            pivot[where, :] = jnp.broadcast_to(
                jnp.mean(blocks[0][:, :128], axis=1, keepdims=True), (size, 128)
            )

        if first is not None:
            pl.when(first)(_)
        base = pivot[where, :]
        one = jnp.zeros((size, 128), F32)
        two = jnp.zeros((size, 128), F32)
        for block in blocks:
            for at in range(0, block.shape[1], 128):
                off = block[:, at : at + 128] - base
                one = one + off
                two = two + off * off
        acc1[where, :] += one
        acc2[where, :] += two

    for k in range(parts):
        pltpu.make_async_copy(
            feat.at[pl.ds(k * 256, 256)], fbuf.at[pl.ds(k * 256, 256)], fsem.at[k]
        ).wait()

        def spread(j, carry, k=k):
            at = pl.ds(pl.multiple_of(j * step, step), step)
            moved = jnp.dot(perm[...], fbuf[k * 256 : (k + 1) * 256, at], preferred_element_type=F32)
            blocks = [moved[r * per : (r + 1) * per] for r in range(rows)]
            for r in range(rows):
                start = (1 + r) * chans + k * per
                xt[start : start + per, at] = blocks[r].astype(BF16)
            accumulate(k * per, blocks, j == 0)
            return carry

        lax.fori_loop(0, chunks, spread, 0)

    pl.semaphore_wait(barrier, greet)

    def halo(buf, turn, side):
        mine, theirs = ((1, rows + 1), (rows, 0))[side]
        return pltpu.make_async_remote_copy(
            src_ref=buf.at[pl.ds(mine * chans, chans)],
            dst_ref=buf.at[pl.ds(theirs * chans, chans)],
            send_sem=hs.at[turn, side],
            recv_sem=hr.at[turn, side],
            device_id={"tile": me_t - 1 if side == 0 else me_t + 1},
            device_id_type=MESH,
        )

    def send_halo(buf, turn, side):
        @pl.when(top if side == 0 else bottom)
        def _():
            halo(buf, turn, side).start()

    def stat_copy(turn, src, dev, d):
        return pltpu.make_async_remote_copy(
            src_ref=stat.at[turn, src],
            dst_ref=stat.at[turn, src],
            send_sem=ssem.at[turn, d],
            recv_sem=rsem.at[turn, src],
            device_id={"tile": dev},
            device_id_type=MESH,
        )

    def fill_weights():
        wide[...] = jnp.zeros_like(wide)
        loads[0].wait()
        loads[1].wait()
        for which, source in enumerate((wa, wb)):
            for out_row in range(2):
                for tap_row in range(3):
                    for tap_col in range(3):
                        at = (out_row + tap_row) * 3 * chans + tap_col * chans
                        wide[which, out_row * chans : (out_row + 1) * chans, at : at + chans] = source[
                            3 * tap_row + tap_col
                        ]

    count = rows * cols

    def norm_values(turn, meanwhile):
        one = jnp.sum(acc1[...], axis=1, keepdims=True)
        two = jnp.sum(acc2[...], axis=1, keepdims=True)
        mean = pivot[:, 0:1] + one / count
        dev2 = jnp.maximum(two - one * one / count, 0.0)
        row_id = lax.broadcasted_iota(jnp.int32, (8, chans), 0)
        stat[turn, me_t] = jnp.where(row_id == 0, lane_to_row(mean), lane_to_row(dev2))
        for d in range(1, tiles):
            stat_copy(turn, me_t, lax.rem(me_t + d, tiles), d).start()
        meanwhile()
        for d in range(1, tiles):
            other = lax.rem(me_t + d, tiles)
            stat_copy(turn, other, other, d).wait_recv()
        size = chans // GROUPS
        group = (
            lax.broadcasted_iota(jnp.int32, (chans, chans), 0) >> log2(size)
            == lax.broadcasted_iota(jnp.int32, (chans, chans), 1) >> log2(size)
        )
        every = [stat[turn, t] for t in range(tiles)]
        total = sum(one_of[0:1, :] for one_of in every)
        gmean = jnp.sum(jnp.where(group, total, 0.0), axis=1, keepdims=True) / (size * tiles)
        dev = jnp.zeros((chans, chans), F32)
        for one_of in every:
            gap = one_of[0:1, :] - gmean
            dev = dev + (one_of[1:2, :] + count * (gap * gap))
        gvar = jnp.sum(jnp.where(group, dev, 0.0), axis=1, keepdims=True) / (size * tiles * count)
        meanb[...] = jnp.broadcast_to(gmean, meanb.shape)
        rstdb[...] = jnp.broadcast_to(0.5 * lax.rsqrt(gvar + EPS), rstdb.shape)
        for d in range(1, tiles):
            stat_copy(turn, me_t, lax.rem(me_t + d, tiles), d).wait_send()

    edge_lane = lax.broadcasted_iota(jnp.int32, (16, 128), 1)
    blocks_of = chans // 16

    def activate_block(src, row, block):
        here = pl.ds(pl.multiple_of(block * 16, 16), 16)
        value = src[pl.ds(pl.multiple_of(row * chans + block * 16, 16), 16), :].astype(F32)
        half = (value - meanb[here, 0:1]) * rstdb[here, 0:1]
        result = (half + half * jnp.tanh(half)).astype(BF16)
        before = pltpu.roll(result, 1, 1)
        after = pltpu.roll(result, cols - 1, 1)
        into = acts[row // 2]
        for tap, one_of in enumerate((before, result, after)):
            start = pl.multiple_of(((row % 2) * 3 + tap) * chans + block * 16, 16)
            into[pl.ds(start, 16), :] = one_of
            if tap != 1:
                lanes = slice(0, 128) if tap == 0 else slice(cols - 128, cols)
                keep = edge_lane != (0 if tap == 0 else 127)
                part = one_of[:, lanes].astype(F32)
                into[pl.ds(start, 16), lanes] = jnp.where(keep, part, 0.0).astype(BF16)

    def activate(src, row):
        def body(block, carry):
            activate_block(src, row, block)
            return carry

        lax.fori_loop(0, blocks_of, body, 0)

    def activate_edge(buf, turn, row):
        side, there = (1, top) if row == 0 else (0, bottom)

        @pl.when(there)
        def _():
            halo(buf, turn, side).wait_recv()
            activate(buf, row)

        @pl.when(jnp.logical_not(there))
        def _():
            start = (row % 2) * 3 * chans
            acts[row // 2][start : start + 3 * chans, :] = jnp.zeros((3 * chans, cols), BF16)

    def finish_halo(buf, turn):
        for side, there in ((0, top), (1, bottom)):
            @pl.when(there)
            def _(side=side):
                halo(buf, turn, side).wait_send()

    def conv(which, p, at):
        half = 6 * chans
        return jnp.dot(wide[which, :, :half], acts[p][:, at], preferred_element_type=F32) + jnp.dot(
            wide[which, :, half:], acts[p + 1][:, at], preferred_element_type=F32
        )

    send_halo(xt, 0, 0)
    send_halo(xt, 0, 1)
    norm_values(0, fill_weights)
    acc1[...] = jnp.zeros_like(acc1)
    acc2[...] = jnp.zeros_like(acc2)

    def first_conv(p, first, beside):
        total = len(beside) * blocks_of // chunks

        def over_cols(j, carry):
            at = pl.ds(pl.multiple_of(j * step, step), step)
            result = conv(0, p, at).astype(BF16)
            for row in beside:
                for n in range(total // len(beside)):
                    activate_block(xt, row, j * (total // len(beside)) + n)
            start = (1 + 2 * p) * chans
            hid[start : start + 2 * chans, at] = result
            wide_result = result.astype(F32)
            accumulate(0, [wide_result[:chans], wide_result[chans:]], (j == 0) if first else None)
            return carry

        lax.fori_loop(0, chunks, over_cols, 0)

    for row in (1, 2, 3):
        activate(xt, row)
    activate_edge(xt, 0, 0)
    first_conv(0, True, [rows - 2, rows - 1, rows])
    send_halo(hid, 1, 0)
    activate_edge(xt, 0, rows + 1)
    middle = list(range(4, rows - 2))
    first_conv(pairs - 1, False, middle)
    send_halo(hid, 1, 1)
    for p in range(1, pairs - 1):
        first_conv(p, False, [])
    norm_values(1, lambda: None)
    for row in range(1, rows + 1):
        activate(hid, row)
    activate_edge(hid, 1, 0)
    activate_edge(hid, 1, rows + 1)
    for load in loads[2:]:
        load.wait()

    at_step = jnp.full((8, 128), coef[0], jnp.int32).astype(F32)
    upper = 800.0 ** (1.0 / 7.0)
    lower = 0.002 ** (1.0 / 7.0)

    def level(place):
        base = upper + place / 17.0 * (lower - upper)
        square = base * base
        return base * square * (square * square)

    sigma = level(at_step)
    sigma_next = level(at_step + 1.0)
    sigma_hat = 1.25 * sigma
    spread_of = jnp.sqrt(sigma_hat * sigma_hat - sigma * sigma)[0:1, 0:1]
    c_skip = (0.25 / (sigma_hat * sigma_hat + 0.25))[0:1, 0:1]
    c_out = (0.5 * sigma_hat / jnp.sqrt(sigma_hat * sigma_hat + 0.25))[0:1, 0:1]
    drift = ((sigma_next - sigma_hat) / sigma_hat)[0:1, 0:1]

    def advance(j):
        at = pl.ds(pl.multiple_of(j * step, step), step)
        network = jnp.zeros((outs * rows, step), F32)
        for p in range(pairs):
            start = (1 + 2 * p) * chans
            block = (xt[start : start + 2 * chans, at].astype(F32) + conv(1, p, at)).astype(BF16)
            network = network + jnp.dot(hw[p], block, preferred_element_type=F32)
        state_hat = resid[:, at] + spread_of * noise[:, at]
        denoised = c_skip * state_hat + c_out * network
        out_next[:, at] = state_hat + drift * (state_hat - denoised)

    if not fused:
        lax.fori_loop(0, chunks, lambda j, c: (advance(j), c)[1], 0)
        finish_halo(xt, 0)
        finish_halo(hid, 1)
        return

    width = cols // members
    ratio = width // step

    def state_copy(owner, sender):
        return pltpu.make_async_remote_copy(
            src_ref=out_next.at[:, pl.ds(pl.multiple_of(owner * width, width), width)],
            dst_ref=ens_in.at[sender],
            send_sem=es.at[owner],
            recv_sem=er.at[sender],
            device_id={"member": owner},
            device_id_type=MESH,
        )

    def back_copy(owner, member):
        return pltpu.make_async_remote_copy(
            src_ref=back_out,
            dst_ref=back_in.at[owner],
            send_sem=bs.at[member],
            recv_sem=br.at[owner],
            device_id={"member": member},
            device_id_type=MESH,
        )

    def ensemble():
        for d in range(1, members):
            other = lax.rem(me_m + d, members)
            state_copy(me_m, other).wait_recv()
        for o in range(outs):
            sub = pl.ds(o * rows, rows)
            one = jnp.zeros((rows, width), F32)
            two = jnp.zeros((rows, width), F32)
            for m in range(members):
                value = ens_in[m, sub, :]
                one = one + value
                two = two + value * value
            mean = one / members
            var = two / members - mean * mean
            factor = jnp.sqrt(1.0 + target[o] / (var + 1.0))
            back_out[0, sub, :] = regr[sub, :] + (mean - mean * factor)
            back_out[1, sub, :] = factor
        for d in range(1, members):
            back_copy(me_m, lax.rem(me_m + d, members)).start()
        mine = pl.ds(pl.multiple_of(me_m * width, width), width)
        out_field[:, mine] = back_out[0] + out_next[:, mine] * back_out[1]

    def turn_of(owner, carry):
        @pl.when(owner < members)
        def _():
            for part in range(ratio):
                advance(owner * ratio + part)

            @pl.when(owner != me_m)
            def _():
                state_copy(owner, me_m).start()

            @pl.when(owner == me_m)
            def _():
                ens_in[me_m] = out_next[:, pl.ds(pl.multiple_of(owner * width, width), width)]

        @pl.when(owner == me_m + 1)
        def _():
            ensemble()

        return carry

    lax.fori_loop(0, members + 1, turn_of, 0)

    def collect(d, carry):
        owner = lax.rem(me_m + d, members)
        back_copy(owner, owner).wait_recv()
        at = pl.ds(pl.multiple_of(owner * width, width), width)
        out_field[:, at] = back_in[owner, 0] + out_next[:, at] * back_in[owner, 1]
        return carry

    lax.fori_loop(1, members, collect, 0)
    for d in range(1, members):
        other = lax.rem(me_m + d, members)
        state_copy(other, me_m).wait_send()
        back_copy(me_m, other).wait_send()
    finish_halo(xt, 0)
    finish_halo(hid, 1)


def shards(
    features,
    residual_state,
    noise,
    regression_mean,
    step_index,
    conv_first,
    conv_second,
    head_weight,
    spread_target,
):
    tiles = lax.axis_size("tile")
    members = lax.axis_size("member")
    _, chans, rows, cols = features.shape
    outs = residual_state.shape[1]
    step = 256
    fused = (cols // members) % step == 0
    flat = outs * rows
    padded = rows + 2
    vmem = pl.BlockSpec(memory_space=pltpu.VMEM)
    smem = pl.BlockSpec(memory_space=pltpu.SMEM)
    anywhere = pl.BlockSpec(memory_space=pl.ANY)
    operands = [
        (smem, step_index),
        (smem, spread_target),
        (anywhere, features.reshape(chans * rows, cols)),
        (anywhere, residual_state.reshape(flat, cols)),
        (anywhere, noise.reshape(flat, cols)),
        (anywhere, regression_mean.reshape(flat, cols // members)),
        (anywhere, conv_first),
        (anywhere, conv_second),
        (vmem, head_weight),
    ]
    if not fused:
        del operands[5]
    dma = pltpu.SemaphoreType.DMA
    scratch = [pltpu.VMEM((6 * chans, cols), BF16) for _ in range(rows // 2 + 1)] + [
        pltpu.VMEM((chans * rows, cols), BF16),
        pltpu.VMEM((padded * chans, cols), BF16),
        pltpu.VMEM((padded * chans, cols), BF16),
        pltpu.VMEM((2, 2 * chans, 12 * chans), BF16),
        pltpu.VMEM((rows // 2, flat, 2 * chans), BF16),
        pltpu.VMEM((256, 256), BF16),
        pltpu.VMEM((chans, 128), F32),
        pltpu.VMEM((chans, 128), F32),
        pltpu.VMEM((chans, 128), F32),
        pltpu.VMEM((chans, 128), F32),
        pltpu.VMEM((chans, 128), F32),
        pltpu.VMEM((2, tiles, 8, chans), F32),
        pltpu.VMEM((flat, cols), F32),
        pltpu.VMEM((flat, cols), F32),
        pltpu.VMEM(conv_first.shape, BF16),
        pltpu.VMEM(conv_second.shape, BF16),
        dma((chans * rows // 256,)),
        dma((2, tiles)),
        dma((2, tiles)),
        dma((2, 2)),
        dma((2, 2)),
        dma((5,)),
    ]
    if fused:
        scratch += [
            pltpu.VMEM((members, flat, cols // members), F32),
            pltpu.VMEM((2, flat, cols // members), F32),
            pltpu.VMEM((members, 2, flat, cols // members), F32),
            pltpu.VMEM((flat, cols // members), F32),
            dma((members,)),
            dma((members,)),
            dma((members,)),
            dma((members,)),
        ]
    result = pl.pallas_call(
        functools.partial(kernel, tiles, members, fused, chans, rows, cols, step),
        out_shape=[jax.ShapeDtypeStruct((flat, cols), F32)] * (2 if fused else 1),
        in_specs=[spec for spec, _ in operands],
        out_specs=[vmem] * (2 if fused else 1),
        scratch_shapes=scratch,
        compiler_params=pltpu.CompilerParams(
            collective_id=0, has_side_effects=True, vmem_limit_bytes=52 * 1024 * 1024
        ),
    )(*[value for _, value in operands])
    advanced = result[0].reshape(outs, rows, cols)
    if fused:
        return (result[1].reshape(1, outs, rows, cols), advanced[None])
    target = spread_target[:, None, None]
    regional = lax.all_gather(regression_mean, "member", axis=2, tiled=True)
    first, second = lax.psum((advanced, advanced * advanced), "member")
    ens_mean = first / members
    ens_var = second / members - ens_mean * ens_mean
    factor = jnp.sqrt(1.0 + target / (ens_var + 1.0))
    field = regional + ens_mean + (advanced - ens_mean) * factor
    return (field[None], advanced[None])


def solution(mesh):
    return jax.shard_map(
        shards,
        mesh=mesh,
        in_specs=(
            P("member", None, "tile", None),
            P("member", None, "tile", None),
            P("member", None, "tile", None),
            P(None, "tile", "member"),
            P(),
            P(),
            P(),
            P(),
            P(),
        ),
        out_specs=(P("member", None, "tile", None), P("member", None, "tile", None)),
        check_vma=False,
    )
```

```python
import functools

import jax
import jax.numpy as jnp
from jax import lax
from jax.experimental import pallas as pl
from jax.experimental.pallas import tpu as pltpu
from jax.sharding import PartitionSpec as P

GROUPS = 32
EPS = 1e-05
F32 = jnp.float32
BF16 = jnp.bfloat16
MESH = pl.DeviceIdType.MESH
LAG = 128


def log2(n):
    assert n & (n - 1) == 0
    return n.bit_length() - 1


def lane_to_row(column):
    n = column.shape[0]
    same = lax.broadcasted_iota(jnp.int32, (n, n), 0) == lax.broadcasted_iota(jnp.int32, (n, n), 1)
    return jnp.sum(jnp.where(same, column, 0.0), axis=0, keepdims=True)


def kernel(tiles, members, fused, chans, rows, cols, step, *refs):
    if fused:
        (coef, target, feat, resid_h, noise_h, regr_h, wa_h, wb_h, head, out_next, out_field) = refs[:11]
        refs = refs[11:]
    else:
        (coef, target, feat, resid_h, noise_h, wa_h, wb_h, head, out_next) = refs[:9]
        refs = refs[9:]
    acts = refs[: rows // 2 + 1]
    refs = refs[rows // 2 + 1 :]
    (fbuf, xt, hid, wide, hw, perm, pivot, acc1, acc2, meanb, rstdb, stat, resid, noise, wa, wb,
     pend, carry_m, state, fsem, ssem, rsem, hs, hr, osem) = refs[:25]
    if fused:
        ens_in, back_out, back_in, regr, field, es, er, bs, br = refs[25:]
    me_t = lax.axis_index("tile")
    me_m = lax.axis_index("member")
    top = me_t > 0
    bottom = me_t < tiles - 1
    chunks = cols // step
    per = 256 // rows
    parts = chans // per
    pairs = rows // 2

    for k in range(parts):
        pltpu.make_async_copy(
            feat.at[pl.ds(k * 256, 256)], fbuf.at[pl.ds(k * 256, 256)], fsem.at[k]
        ).start()
    inner = pl.ds(LAG, cols)
    pairs_of = [(wa_h, wa), (wb_h, wb), (resid_h, resid.at[:, inner]), (noise_h, noise.at[:, inner])]
    if fused:
        pairs_of.append((regr_h, regr))
    loads = [pltpu.make_async_copy(a, b, osem.at[n]) for n, (a, b) in enumerate(pairs_of)]
    for load in loads:
        load.start()

    barrier = pltpu.get_barrier_semaphore()
    for d in range(1, tiles):
        pl.semaphore_signal(barrier, inc=1, device_id={"tile": lax.rem(me_t + d, tiles)}, device_id_type=MESH)
    greet = tiles - 1
    if fused:
        for d in range(1, members):
            pl.semaphore_signal(
                barrier, inc=1, device_id={"member": lax.rem(me_m + d, members)}, device_id_type=MESH
            )
        greet += members - 1

    hw[...] = jnp.zeros_like(hw)
    outs = head.shape[0]
    head32 = head[...].astype(F32)
    for p in range(pairs):
        for out_row in range(2):
            place = lax.broadcasted_iota(jnp.int32, (rows, chans), 0) == 2 * p + out_row
            for o in range(outs):
                hw[p, o * rows : (o + 1) * rows, out_row * chans : (out_row + 1) * chans] = jnp.where(
                    place, head32[o : o + 1, :], 0.0
                ).astype(BF16)
    to = lax.broadcasted_iota(jnp.int32, (256, 256), 0)
    frm = lax.broadcasted_iota(jnp.int32, (256, 256), 1)
    perm[...] = jnp.where((to & (per - 1)) * rows + (to >> log2(per)) == frm, 1.0, 0.0).astype(BF16)
    acc1[...] = jnp.zeros_like(acc1)
    acc2[...] = jnp.zeros_like(acc2)

    def fold(values):
        total = values[:, :128]
        for at in range(128, values.shape[1], 128):
            total = total + values[:, at : at + 128]
        return total

    def accumulate(start, blocks, first):
        size = blocks[0].shape[0]
        where = pl.ds(start, size)

        def _():
            pivot[where, :] = jnp.broadcast_to(
                jnp.mean(blocks[0][:, :128], axis=1, keepdims=True), (size, 128)
            )

        if first is True:
            _()
        elif first is not None:
            pl.when(first)(_)
        base = pivot[where, :]
        one = jnp.zeros((size, 128), F32)
        two = jnp.zeros((size, 128), F32)
        for block in blocks:
            for at in range(0, block.shape[1], 128):
                off = block[:, at : at + 128] - base
                one = one + off
                two = two + off * off
        acc1[where, :] += one
        acc2[where, :] += two

    for k in range(parts):
        pltpu.make_async_copy(
            feat.at[pl.ds(k * 256, 256)], fbuf.at[pl.ds(k * 256, 256)], fsem.at[k]
        ).wait()

        def spread(j, carry, k=k):
            at = pl.ds(pl.multiple_of(j * step, step), step)
            moved = jnp.dot(perm[...], fbuf[k * 256 : (k + 1) * 256, at], preferred_element_type=F32)
            blocks = [moved[r * per : (r + 1) * per] for r in range(rows)]
            for r in range(rows):
                start = (1 + r) * chans + k * per
                xt[start : start + per, pl.ds(pl.multiple_of(j * step + LAG, LAG), step)] = blocks[r].astype(BF16)
            accumulate(k * per, blocks, j == 0)
            return carry

        lax.fori_loop(0, chunks, spread, 0)

    pl.semaphore_wait(barrier, greet)

    def halo(buf, turn, side):
        mine, theirs = ((1, rows + 1), (rows, 0))[side]
        return pltpu.make_async_remote_copy(
            src_ref=buf.at[pl.ds(mine * chans, chans), pl.ds(LAG, cols)],
            dst_ref=buf.at[pl.ds(theirs * chans, chans), pl.ds(LAG, cols)],
            send_sem=hs.at[turn, side],
            recv_sem=hr.at[turn, side],
            device_id={"tile": me_t - 1 if side == 0 else me_t + 1},
            device_id_type=MESH,
        )

    def send_halo(buf, turn, side):
        @pl.when(top if side == 0 else bottom)
        def _():
            halo(buf, turn, side).start()

    def stat_copy(turn, src, dev, d):
        return pltpu.make_async_remote_copy(
            src_ref=stat.at[turn, src],
            dst_ref=stat.at[turn, src],
            send_sem=ssem.at[turn, d],
            recv_sem=rsem.at[turn, src],
            device_id={"tile": dev},
            device_id_type=MESH,
        )

    def fill_weights():
        wide[...] = jnp.zeros_like(wide)
        loads[0].wait()
        loads[1].wait()
        for which, source in enumerate((wa, wb)):
            for out_row in range(2):
                for tap_row in range(3):
                    for tap_col in range(3):
                        at = (out_row + tap_row) * chans
                        to_row = (2 * tap_col + out_row) * chans
                        wide[which, to_row : to_row + chans, at : at + chans] = source[
                            3 * tap_row + tap_col
                        ]

    count = rows * cols

    def norm_values(turn, meanwhile):
        one = jnp.sum(acc1[...], axis=1, keepdims=True)
        two = jnp.sum(acc2[...], axis=1, keepdims=True)
        mean = pivot[:, 0:1] + one / count
        dev2 = jnp.maximum(two - one * one / count, 0.0)
        row_id = lax.broadcasted_iota(jnp.int32, (8, chans), 0)
        stat[turn, me_t] = jnp.where(row_id == 0, lane_to_row(mean), lane_to_row(dev2))
        for d in range(1, tiles):
            stat_copy(turn, me_t, lax.rem(me_t + d, tiles), d).start()
        meanwhile()
        for d in range(1, tiles):
            other = lax.rem(me_t + d, tiles)
            stat_copy(turn, other, other, d).wait_recv()
        size = chans // GROUPS
        group = (
            lax.broadcasted_iota(jnp.int32, (chans, chans), 0) >> log2(size)
            == lax.broadcasted_iota(jnp.int32, (chans, chans), 1) >> log2(size)
        )
        every = [stat[turn, t] for t in range(tiles)]
        total = sum(one_of[0:1, :] for one_of in every)
        gmean = jnp.sum(jnp.where(group, total, 0.0), axis=1, keepdims=True) / (size * tiles)
        dev = jnp.zeros((chans, chans), F32)
        for one_of in every:
            gap = one_of[0:1, :] - gmean
            dev = dev + (one_of[1:2, :] + count * (gap * gap))
        gvar = jnp.sum(jnp.where(group, dev, 0.0), axis=1, keepdims=True) / (size * tiles * count)
        meanb[...] = jnp.broadcast_to(gmean, meanb.shape)
        rstdb[...] = jnp.broadcast_to(0.5 * lax.rsqrt(gvar + EPS), rstdb.shape)
        for d in range(1, tiles):
            stat_copy(turn, me_t, lax.rem(me_t + d, tiles), d).wait_send()

    blocks_of = chans // 16

    def activate_block(src, row, block):
        here = pl.ds(pl.multiple_of(block * 16, 16), 16)
        value = src[pl.ds(pl.multiple_of(row * chans + block * 16, 16), 16), LAG:].astype(F32)
        half = (value - meanb[here, 0:1]) * rstdb[here, 0:1]
        start = pl.multiple_of((row % 2) * chans + block * 16, 16)
        acts[row // 2][pl.ds(start, 16), :] = (half + half * jnp.tanh(half)).astype(BF16)

    def activate(src, row):
        def body(block, carry):
            activate_block(src, row, block)
            return carry

        lax.fori_loop(0, blocks_of, body, 0)

    def activate_edge(buf, turn, row):
        side, there = (1, top) if row == 0 else (0, bottom)

        @pl.when(there)
        def _():
            halo(buf, turn, side).wait_recv()
            activate(buf, row)

        @pl.when(jnp.logical_not(there))
        def _():
            start = (row % 2) * chans
            acts[row // 2][start : start + chans, :] = jnp.zeros((chans, cols), BF16)

    def finish_halo(buf, turn):
        for side, there in ((0, top), (1, bottom)):
            @pl.when(there)
            def _(side=side):
                halo(buf, turn, side).wait_send()

    lane = lax.broadcasted_iota(jnp.int32, (2 * chans, LAG), 1)

    def conv(which, p, slot, at):
        taps = jnp.dot(
            wide[which],
            jnp.concatenate([acts[p][:, at], acts[p + 1][:, at]], axis=0),
            preferred_element_type=F32,
        )
        left, centre, right = (taps[n * 2 * chans : (n + 1) * 2 * chans] for n in range(3))
        left0, left1 = (pltpu.roll(left[:, n : n + LAG], 1, 1) for n in (0, LAG))
        right0, right1 = (pltpu.roll(right[:, n : n + LAG], LAG - 1, 1) for n in (0, LAG))
        before = pend[slot] + jnp.where(lane == LAG - 1, right0, 0.0)
        first = (
            centre[:, :LAG]
            + jnp.where(lane == 0, carry_m[slot], left0)
            + jnp.where(lane == LAG - 1, right1, right0)
        )
        pend[slot] = (
            centre[:, LAG:]
            + jnp.where(lane == 0, left0, left1)
            + jnp.where(lane == LAG - 1, 0.0, right1)
        )
        carry_m[slot] = left1
        return before, first

    send_halo(xt, 0, 0)
    send_halo(xt, 0, 1)
    norm_values(0, fill_weights)
    acc1[...] = jnp.zeros_like(acc1)
    acc2[...] = jnp.zeros_like(acc2)

    def first_conv(p, first, beside):
        each = blocks_of // chunks
        rows_at = slice((1 + 2 * p) * chans, (3 + 2 * p) * chans)
        pend[0] = jnp.zeros_like(pend[0])
        carry_m[0] = jnp.zeros_like(carry_m[0])

        def keep(blocks, starts, pivot_now):
            kept = []
            for block, start in zip(blocks, starts):
                rounded = block.astype(BF16)
                hid[rows_at, pl.ds(start, LAG)] = rounded
                wide_block = rounded.astype(F32)
                kept += [wide_block[:chans], wide_block[chans:]]
            accumulate(0, kept, pivot_now)

        def over_cols(j, carry):
            base = j * step
            if not isinstance(j, int):
                base = pl.multiple_of(base, step)
            blocks = conv(0, p, 0, pl.ds(base, step))
            for row in beside:
                for n in range(each):
                    activate_block(xt, row, j * each + n)
            if isinstance(j, int):
                keep(blocks[1:], [LAG], True if first else None)
            else:
                keep(blocks, [base, pl.multiple_of(base + LAG, LAG)], None)
            return carry

        over_cols(0, 0)
        lax.fori_loop(1, chunks, over_cols, 0)
        keep([pend[0]], [cols], None)

    for row in (1, 2, 3):
        activate(xt, row)
    activate_edge(xt, 0, 0)
    first_conv(0, True, [rows - 2, rows - 1, rows])
    send_halo(hid, 1, 0)
    activate_edge(xt, 0, rows + 1)
    middle = list(range(4, rows - 2))
    first_conv(pairs - 1, False, middle)
    send_halo(hid, 1, 1)
    for p in range(1, pairs - 1):
        first_conv(p, False, [])
    norm_values(1, lambda: None)
    for row in range(1, rows + 1):
        activate(hid, row)
    activate_edge(hid, 1, 0)
    activate_edge(hid, 1, rows + 1)
    for load in loads[2:]:
        load.wait()

    at_step = jnp.full((8, 128), coef[0], jnp.int32).astype(F32)
    upper = 800.0 ** (1.0 / 7.0)
    lower = 0.002 ** (1.0 / 7.0)

    def level(place):
        base = upper + place / 17.0 * (lower - upper)
        square = base * base
        return base * square * (square * square)

    sigma = level(at_step)
    sigma_next = level(at_step + 1.0)
    sigma_hat = 1.25 * sigma
    spread_of = jnp.sqrt(sigma_hat * sigma_hat - sigma * sigma)[0:1, 0:1]
    c_skip = (0.25 / (sigma_hat * sigma_hat + 0.25))[0:1, 0:1]
    c_out = (0.5 * sigma_hat / jnp.sqrt(sigma_hat * sigma_hat + 0.25))[0:1, 0:1]
    drift = ((sigma_next - sigma_hat) / sigma_hat)[0:1, 0:1]

    def advance(blocks_of_pair, start, size):
        at = pl.ds(start, size)
        network = jnp.zeros((outs * rows, size), F32)
        for p in range(pairs):
            first_row = (1 + 2 * p) * chans
            block = (xt[first_row : first_row + 2 * chans, at].astype(F32) + blocks_of_pair(p)).astype(BF16)
            network = network + jnp.dot(hw[p], block, preferred_element_type=F32)
        state_hat = resid[:, at] + spread_of * noise[:, at]
        denoised = c_skip * state_hat + c_out * network
        state[:, at] = state_hat + drift * (state_hat - denoised)

    pend[...] = jnp.zeros_like(pend)
    carry_m[...] = jnp.zeros_like(carry_m)

    def window(j):
        base = pl.multiple_of(j * step, step)
        advance(lambda p: jnp.concatenate(conv(1, p, p, pl.ds(base, step)), axis=1), base, step)

    def last_window():
        advance(lambda p: pend[p], cols, LAG)

    def state_out():
        return pltpu.make_async_copy(state.at[:, inner], out_next, osem.at[0])

    if not fused:
        lax.fori_loop(0, chunks, lambda j, c: (window(j), c)[1], 0)
        last_window()
        state_out().start()
        state_out().wait()
        finish_halo(xt, 0)
        finish_halo(hid, 1)
        return

    width = cols // members
    ratio = width // step

    def owned(owner):
        start = owner * width + LAG
        if not isinstance(start, int):
            start = pl.multiple_of(start, LAG)
        return pl.ds(start, width)

    def state_copy(owner, sender):
        return pltpu.make_async_remote_copy(
            src_ref=state.at[:, owned(owner)],
            dst_ref=ens_in.at[sender],
            send_sem=es.at[owner],
            recv_sem=er.at[sender],
            device_id={"member": owner},
            device_id_type=MESH,
        )

    def back_copy(owner, member):
        return pltpu.make_async_remote_copy(
            src_ref=back_out,
            dst_ref=back_in.at[owner],
            send_sem=bs.at[member],
            recv_sem=br.at[owner],
            device_id={"member": member},
            device_id_type=MESH,
        )

    def ensemble():
        for d in range(1, members):
            other = lax.rem(me_m + d, members)
            state_copy(me_m, other).wait_recv()
        for o in range(outs):
            sub = pl.ds(o * rows, rows)
            one = jnp.zeros((rows, width), F32)
            two = jnp.zeros((rows, width), F32)
            for m in range(members):
                value = ens_in[m, sub, :]
                one = one + value
                two = two + value * value
            mean = one / members
            var = two / members - mean * mean
            factor = jnp.sqrt(1.0 + target[o] / (var + 1.0))
            back_out[0, sub, :] = regr[sub, :] + (mean - mean * factor)
            back_out[1, sub, :] = factor
        for d in range(1, members):
            back_copy(me_m, lax.rem(me_m + d, members)).start()
        mine = pl.ds(pl.multiple_of(me_m * width, width), width)
        field[:, mine] = back_out[0] + state[:, owned(me_m)] * back_out[1]

    def hand_over(owner):
        @pl.when(owner != me_m)
        def _():
            state_copy(owner, me_m).start()

        @pl.when(owner == me_m)
        def _():
            ens_in[me_m] = state[:, owned(owner)]

    def turn_of(j, carry):
        window(j)

        @pl.when((j >= ratio) & (j % ratio == 0))
        def _():
            hand_over(j // ratio - 1)

        @pl.when(j == (me_m + 1) * ratio + 1)
        def _():
            ensemble()

        return carry

    lax.fori_loop(0, chunks, turn_of, 0)
    last_window()
    hand_over(members - 1)

    @pl.when((me_m + 1) * ratio + 1 >= chunks)
    def _():
        ensemble()

    state_out().start()

    def collect(d, carry):
        owner = lax.rem(me_m + d, members)
        back_copy(owner, owner).wait_recv()
        at = pl.ds(pl.multiple_of(owner * width, width), width)
        field[:, at] = back_in[owner, 0] + state[:, owned(owner)] * back_in[owner, 1]
        return carry

    lax.fori_loop(1, members, collect, 0)
    field_out = pltpu.make_async_copy(field, out_field, osem.at[1])
    field_out.start()
    for d in range(1, members):
        other = lax.rem(me_m + d, members)
        state_copy(other, me_m).wait_send()
        back_copy(me_m, other).wait_send()
    finish_halo(xt, 0)
    finish_halo(hid, 1)
    state_out().wait()
    field_out.wait()


def shards(
    features,
    residual_state,
    noise,
    regression_mean,
    step_index,
    conv_first,
    conv_second,
    head_weight,
    spread_target,
):
    tiles = lax.axis_size("tile")
    members = lax.axis_size("member")
    _, chans, rows, cols = features.shape
    outs = residual_state.shape[1]
    step = 256
    fused = (cols // members) % step == 0
    flat = outs * rows
    padded = rows + 2
    vmem = pl.BlockSpec(memory_space=pltpu.VMEM)
    smem = pl.BlockSpec(memory_space=pltpu.SMEM)
    anywhere = pl.BlockSpec(memory_space=pl.ANY)
    operands = [
        (smem, step_index),
        (smem, spread_target),
        (anywhere, features.reshape(chans * rows, cols)),
        (anywhere, residual_state.reshape(flat, cols)),
        (anywhere, noise.reshape(flat, cols)),
        (anywhere, regression_mean.reshape(flat, cols // members)),
        (anywhere, conv_first),
        (anywhere, conv_second),
        (vmem, head_weight),
    ]
    if not fused:
        del operands[5]
    dma = pltpu.SemaphoreType.DMA
    scratch = [pltpu.VMEM((2 * chans, cols), BF16) for _ in range(rows // 2 + 1)] + [
        pltpu.VMEM((chans * rows, cols), BF16),
        pltpu.VMEM((padded * chans, LAG + cols), BF16),
        pltpu.VMEM((padded * chans, LAG + cols), BF16),
        pltpu.VMEM((2, 6 * chans, 4 * chans), BF16),
        pltpu.VMEM((rows // 2, flat, 2 * chans), BF16),
        pltpu.VMEM((256, 256), BF16),
        pltpu.VMEM((chans, 128), F32),
        pltpu.VMEM((chans, 128), F32),
        pltpu.VMEM((chans, 128), F32),
        pltpu.VMEM((chans, 128), F32),
        pltpu.VMEM((chans, 128), F32),
        pltpu.VMEM((2, tiles, 8, chans), F32),
        pltpu.VMEM((flat, LAG + cols), F32),
        pltpu.VMEM((flat, LAG + cols), F32),
        pltpu.VMEM(conv_first.shape, BF16),
        pltpu.VMEM(conv_second.shape, BF16),
        pltpu.VMEM((rows // 2, 2 * chans, LAG), F32),
        pltpu.VMEM((rows // 2, 2 * chans, LAG), F32),
        pltpu.VMEM((flat, LAG + cols), F32),
        dma((chans * rows // 256,)),
        dma((2, tiles)),
        dma((2, tiles)),
        dma((2, 2)),
        dma((2, 2)),
        dma((5,)),
    ]
    if fused:
        scratch += [
            pltpu.VMEM((members, flat, cols // members), F32),
            pltpu.VMEM((2, flat, cols // members), F32),
            pltpu.VMEM((members, 2, flat, cols // members), F32),
            pltpu.VMEM((flat, cols // members), F32),
            pltpu.VMEM((flat, cols), F32),
            dma((members,)),
            dma((members,)),
            dma((members,)),
            dma((members,)),
        ]
    result = pl.pallas_call(
        functools.partial(kernel, tiles, members, fused, chans, rows, cols, step),
        out_shape=[jax.ShapeDtypeStruct((flat, cols), F32)] * (2 if fused else 1),
        in_specs=[spec for spec, _ in operands],
        out_specs=[anywhere] * (2 if fused else 1),
        scratch_shapes=scratch,
        compiler_params=pltpu.CompilerParams(
            collective_id=0, has_side_effects=True, vmem_limit_bytes=52 * 1024 * 1024
        ),
    )(*[value for _, value in operands])
    advanced = result[0].reshape(outs, rows, cols)
    if fused:
        return (result[1].reshape(1, outs, rows, cols), advanced[None])
    target = spread_target[:, None, None]
    regional = lax.all_gather(regression_mean, "member", axis=2, tiled=True)
    first, second = lax.psum((advanced, advanced * advanced), "member")
    ens_mean = first / members
    ens_var = second / members - ens_mean * ens_mean
    factor = jnp.sqrt(1.0 + target / (ens_var + 1.0))
    field = regional + ens_mean + (advanced - ens_mean) * factor
    return (field[None], advanced[None])


def solution(mesh):
    return jax.shard_map(
        shards,
        mesh=mesh,
        in_specs=(
            P("member", None, "tile", None),
            P("member", None, "tile", None),
            P("member", None, "tile", None),
            P(None, "tile", "member"),
            P(),
            P(),
            P(),
            P(),
            P(),
        ),
        out_specs=(P("member", None, "tile", None), P("member", None, "tile", None)),
        check_vma=False,
    )
```

```python
import functools

import jax
import jax.numpy as jnp
from jax import lax
from jax.experimental import pallas as pl
from jax.experimental.pallas import tpu as pltpu
from jax.sharding import PartitionSpec as P

GROUPS = 32
EPS = 1e-05
F32 = jnp.float32
BF16 = jnp.bfloat16
MESH = pl.DeviceIdType.MESH
LAG = 128


def log2(n):
    assert n & (n - 1) == 0
    return n.bit_length() - 1


def lane_to_row(column):
    n = column.shape[0]
    same = lax.broadcasted_iota(jnp.int32, (n, n), 0) == lax.broadcasted_iota(jnp.int32, (n, n), 1)
    return jnp.sum(jnp.where(same, column, 0.0), axis=0, keepdims=True)


def kernel(tiles, members, fused, chans, rows, cols, step, *refs):
    if fused:
        (coef, target, feat, resid_h, noise_h, regr_h, wa_h, wb_h, head, out_next, out_field) = refs[:11]
        refs = refs[11:]
    else:
        (coef, target, feat, resid_h, noise_h, wa_h, wb_h, head, out_next) = refs[:9]
        refs = refs[9:]
    acts = refs[: rows // 2 + 1]
    refs = refs[rows // 2 + 1 :]
    (fbuf, xt, hid, wide, hw, perm, pivot, acc1, acc2, meanb, rstdb, stat, resid, noise, wa, wb,
     pend, carry_m, state, fsem, ssem, rsem, hs, hr, osem) = refs[:25]
    if fused:
        ens_in, back_out, back_in, regr, field, es, er, bs, br = refs[25:]
    me_t = lax.axis_index("tile")
    me_m = lax.axis_index("member")
    top = me_t > 0
    bottom = me_t < tiles - 1
    chunks = cols // step
    per = 256 // rows
    parts = chans // per
    pairs = rows // 2

    for k in range(parts):
        pltpu.make_async_copy(
            feat.at[pl.ds(k * 256, 256)], fbuf.at[pl.ds(k * 256, 256)], fsem.at[k]
        ).start()
    inner = pl.ds(LAG, cols)
    pairs_of = [(wa_h, wa), (wb_h, wb), (resid_h, resid.at[:, inner]), (noise_h, noise.at[:, inner])]
    if fused:
        pairs_of.append((regr_h, regr))
    loads = [pltpu.make_async_copy(a, b, osem.at[n]) for n, (a, b) in enumerate(pairs_of)]
    for load in loads:
        load.start()

    barrier = pltpu.get_barrier_semaphore()
    for d in range(1, tiles):
        pl.semaphore_signal(barrier, inc=1, device_id={"tile": lax.rem(me_t + d, tiles)}, device_id_type=MESH)
    greet = tiles - 1
    if fused:
        for d in range(1, members):
            pl.semaphore_signal(
                barrier, inc=1, device_id={"member": lax.rem(me_m + d, members)}, device_id_type=MESH
            )
        greet += members - 1

    hw[...] = jnp.zeros_like(hw)
    outs = head.shape[0]
    head32 = head[...].astype(F32)
    for p in range(pairs):
        for out_row in range(2):
            place = lax.broadcasted_iota(jnp.int32, (rows, chans), 0) == 2 * p + out_row
            for o in range(outs):
                hw[p, o * rows : (o + 1) * rows, out_row * chans : (out_row + 1) * chans] = jnp.where(
                    place, head32[o : o + 1, :], 0.0
                ).astype(BF16)
    to = lax.broadcasted_iota(jnp.int32, (256, 256), 0)
    frm = lax.broadcasted_iota(jnp.int32, (256, 256), 1)
    perm[...] = jnp.where((to & (per - 1)) * rows + (to >> log2(per)) == frm, 1.0, 0.0).astype(BF16)
    acc1[...] = jnp.zeros_like(acc1)
    acc2[...] = jnp.zeros_like(acc2)

    def fold(values):
        total = values[:, :128]
        for at in range(128, values.shape[1], 128):
            total = total + values[:, at : at + 128]
        return total

    def set_pivot(start, block):
        size = block.shape[0]
        pivot[pl.ds(start, size), :] = jnp.broadcast_to(
            jnp.mean(block[:, :128], axis=1, keepdims=True), (size, 128)
        )

    def accumulate(start, blocks):
        size = blocks[0].shape[0]
        where = pl.ds(start, size)
        base = pivot[where, :]
        one = jnp.zeros((size, 128), F32)
        two = jnp.zeros((size, 128), F32)
        for block in blocks:
            for at in range(0, block.shape[1], 128):
                off = block[:, at : at + 128] - base
                one = one + off
                two = two + off * off
        acc1[where, :] += one
        acc2[where, :] += two

    for k in range(parts):
        pltpu.make_async_copy(
            feat.at[pl.ds(k * 256, 256)], fbuf.at[pl.ds(k * 256, 256)], fsem.at[k]
        ).wait()

        def spread(j, carry, k=k):
            at = pl.ds(pl.multiple_of(j * step, step), step)
            moved = jnp.dot(perm[...], fbuf[k * 256 : (k + 1) * 256, at], preferred_element_type=F32)
            blocks = [moved[r * per : (r + 1) * per] for r in range(rows)]
            for r in range(rows):
                start = (1 + r) * chans + k * per
                xt[start : start + per, pl.ds(pl.multiple_of(j * step + LAG, LAG), step)] = blocks[r].astype(BF16)
            accumulate(k * per, blocks)
            return carry

        ahead = jnp.dot(
            perm[...], fbuf[k * 256 : (k + 1) * 256, 0:128], preferred_element_type=F32
        )
        set_pivot(k * per, ahead[:per])
        lax.fori_loop(0, chunks, spread, 0, unroll=4)

    pl.semaphore_wait(barrier, greet)

    def halo(buf, turn, side):
        mine, theirs = ((1, rows + 1), (rows, 0))[side]
        return pltpu.make_async_remote_copy(
            src_ref=buf.at[pl.ds(mine * chans, chans), pl.ds(LAG, cols)],
            dst_ref=buf.at[pl.ds(theirs * chans, chans), pl.ds(LAG, cols)],
            send_sem=hs.at[turn, side],
            recv_sem=hr.at[turn, side],
            device_id={"tile": me_t - 1 if side == 0 else me_t + 1},
            device_id_type=MESH,
        )

    def send_halo(buf, turn, side):
        @pl.when(top if side == 0 else bottom)
        def _():
            halo(buf, turn, side).start()

    def stat_copy(turn, src, dev, d):
        return pltpu.make_async_remote_copy(
            src_ref=stat.at[turn, src],
            dst_ref=stat.at[turn, src],
            send_sem=ssem.at[turn, d],
            recv_sem=rsem.at[turn, src],
            device_id={"tile": dev},
            device_id_type=MESH,
        )

    def fill_weights():
        wide[...] = jnp.zeros_like(wide)
        loads[0].wait()
        loads[1].wait()
        for which, source in enumerate((wa, wb)):
            for out_row in range(2):
                for tap_row in range(3):
                    for tap_col in range(3):
                        at = (out_row + tap_row) * chans
                        to_row = (2 * tap_col + out_row) * chans
                        wide[which, to_row : to_row + chans, at : at + chans] = source[
                            3 * tap_row + tap_col
                        ]

    count = rows * cols

    def norm_values(turn, meanwhile):
        one = jnp.sum(acc1[...], axis=1, keepdims=True)
        two = jnp.sum(acc2[...], axis=1, keepdims=True)
        mean = pivot[:, 0:1] + one / count
        dev2 = jnp.maximum(two - one * one / count, 0.0)
        row_id = lax.broadcasted_iota(jnp.int32, (8, chans), 0)
        stat[turn, me_t] = jnp.where(row_id == 0, lane_to_row(mean), lane_to_row(dev2))
        for d in range(1, tiles):
            stat_copy(turn, me_t, lax.rem(me_t + d, tiles), d).start()
        meanwhile()
        for d in range(1, tiles):
            other = lax.rem(me_t + d, tiles)
            stat_copy(turn, other, other, d).wait_recv()
        size = chans // GROUPS
        group = (
            lax.broadcasted_iota(jnp.int32, (chans, chans), 0) >> log2(size)
            == lax.broadcasted_iota(jnp.int32, (chans, chans), 1) >> log2(size)
        )
        every = [stat[turn, t] for t in range(tiles)]
        total = sum(one_of[0:1, :] for one_of in every)
        gmean = jnp.sum(jnp.where(group, total, 0.0), axis=1, keepdims=True) / (size * tiles)
        dev = jnp.zeros((chans, chans), F32)
        for one_of in every:
            gap = one_of[0:1, :] - gmean
            dev = dev + (one_of[1:2, :] + count * (gap * gap))
        gvar = jnp.sum(jnp.where(group, dev, 0.0), axis=1, keepdims=True) / (size * tiles * count)
        meanb[...] = jnp.broadcast_to(gmean, meanb.shape)
        rstdb[...] = jnp.broadcast_to(0.5 * lax.rsqrt(gvar + EPS), rstdb.shape)
        for d in range(1, tiles):
            stat_copy(turn, me_t, lax.rem(me_t + d, tiles), d).wait_send()

    blocks_of = chans // 16

    def activate_block(src, row, block):
        here = pl.ds(pl.multiple_of(block * 16, 16), 16)
        value = src[pl.ds(pl.multiple_of(row * chans + block * 16, 16), 16), LAG:].astype(F32)
        half = (value - meanb[here, 0:1]) * rstdb[here, 0:1]
        start = pl.multiple_of((row % 2) * chans + block * 16, 16)
        acts[row // 2][pl.ds(start, 16), :] = (half + half * jnp.tanh(half)).astype(BF16)

    def activate(src, row):
        def body(block, carry):
            activate_block(src, row, block)
            return carry

        lax.fori_loop(0, blocks_of, body, 0, unroll=2)

    def activate_edge(buf, turn, row):
        side, there = (1, top) if row == 0 else (0, bottom)

        @pl.when(there)
        def _():
            halo(buf, turn, side).wait_recv()
            activate(buf, row)

        @pl.when(jnp.logical_not(there))
        def _():
            start = (row % 2) * chans
            acts[row // 2][start : start + chans, :] = jnp.zeros((chans, cols), BF16)

    def finish_halo(buf, turn):
        for side, there in ((0, top), (1, bottom)):
            @pl.when(there)
            def _(side=side):
                halo(buf, turn, side).wait_send()

    lane = lax.broadcasted_iota(jnp.int32, (2 * chans, LAG), 1)

    def conv(which, p, slot, at):
        taps = jnp.dot(
            wide[which],
            jnp.concatenate([acts[p][:, at], acts[p + 1][:, at]], axis=0),
            preferred_element_type=F32,
        )
        left, centre, right = (taps[n * 2 * chans : (n + 1) * 2 * chans] for n in range(3))
        left0, left1 = (pltpu.roll(left[:, n : n + LAG], 1, 1) for n in (0, LAG))
        right0, right1 = (pltpu.roll(right[:, n : n + LAG], LAG - 1, 1) for n in (0, LAG))
        before = pend[slot] + jnp.where(lane == LAG - 1, right0, 0.0)
        first = (
            centre[:, :LAG]
            + jnp.where(lane == 0, carry_m[slot], left0)
            + jnp.where(lane == LAG - 1, right1, right0)
        )
        pend[slot] = (
            centre[:, LAG:]
            + jnp.where(lane == 0, left0, left1)
            + jnp.where(lane == LAG - 1, 0.0, right1)
        )
        carry_m[slot] = left1
        return before, first

    send_halo(xt, 0, 0)
    send_halo(xt, 0, 1)
    norm_values(0, fill_weights)
    acc1[...] = jnp.zeros_like(acc1)
    acc2[...] = jnp.zeros_like(acc2)

    def first_conv(p, first, beside):
        each = blocks_of // chunks
        rows_at = slice((1 + 2 * p) * chans, (3 + 2 * p) * chans)
        pend[0] = jnp.zeros_like(pend[0])
        carry_m[0] = jnp.zeros_like(carry_m[0])

        def keep(blocks, starts, pivot_now):
            kept = []
            for block, start in zip(blocks, starts):
                rounded = block.astype(BF16)
                hid[rows_at, pl.ds(start, LAG)] = rounded
                wide_block = rounded.astype(F32)
                kept += [wide_block[:chans], wide_block[chans:]]
            if pivot_now:
                set_pivot(0, kept[0])
            accumulate(0, kept)

        def over_cols(j, carry):
            base = j * step
            if not isinstance(j, int):
                base = pl.multiple_of(base, step)
            blocks = conv(0, p, 0, pl.ds(base, step))
            for row in beside:
                for n in range(each):
                    activate_block(xt, row, j * each + n)
            if isinstance(j, int) and j == 0:
                keep(blocks[1:], [LAG], first)
            else:
                keep(blocks, [base, base + LAG if isinstance(j, int) else pl.multiple_of(base + LAG, LAG)], False)
            return carry

        def two_chunks(n, carry):
            return over_cols(2 * n + 1, over_cols(2 * n, carry))

        over_cols(1, over_cols(0, 0))
        lax.fori_loop(1, chunks // 2, two_chunks, 0)
        keep([pend[0]], [cols], False)

    for row in (1, 2, 3):
        activate(xt, row)
    activate_edge(xt, 0, 0)
    first_conv(0, True, [rows - 2, rows - 1, rows])
    send_halo(hid, 1, 0)
    activate_edge(xt, 0, rows + 1)
    middle = list(range(4, rows - 2))
    first_conv(pairs - 1, False, middle)
    send_halo(hid, 1, 1)
    for p in range(1, pairs - 1):
        first_conv(p, False, [])
    norm_values(1, lambda: None)
    for row in range(1, rows + 1):
        activate(hid, row)
    activate_edge(hid, 1, 0)
    activate_edge(hid, 1, rows + 1)
    for load in loads[2:]:
        load.wait()

    at_step = jnp.full((8, 128), coef[0], jnp.int32).astype(F32)
    upper = 800.0 ** (1.0 / 7.0)
    lower = 0.002 ** (1.0 / 7.0)

    def level(place):
        base = upper + place / 17.0 * (lower - upper)
        square = base * base
        return base * square * (square * square)

    sigma = level(at_step)
    sigma_next = level(at_step + 1.0)
    sigma_hat = 1.25 * sigma
    spread_of = jnp.sqrt(sigma_hat * sigma_hat - sigma * sigma)[0:1, 0:1]
    c_skip = (0.25 / (sigma_hat * sigma_hat + 0.25))[0:1, 0:1]
    c_out = (0.5 * sigma_hat / jnp.sqrt(sigma_hat * sigma_hat + 0.25))[0:1, 0:1]
    drift = ((sigma_next - sigma_hat) / sigma_hat)[0:1, 0:1]

    def advance(blocks_of_pair, start, size):
        at = pl.ds(start, size)
        network = jnp.zeros((outs * rows, size), F32)
        for p in range(pairs):
            first_row = (1 + 2 * p) * chans
            block = (xt[first_row : first_row + 2 * chans, at].astype(F32) + blocks_of_pair(p)).astype(BF16)
            network = network + jnp.dot(hw[p], block, preferred_element_type=F32)
        state_hat = resid[:, at] + spread_of * noise[:, at]
        denoised = c_skip * state_hat + c_out * network
        state[:, at] = state_hat + drift * (state_hat - denoised)

    pend[...] = jnp.zeros_like(pend)
    carry_m[...] = jnp.zeros_like(carry_m)

    def window(j):
        base = pl.multiple_of(j * step, step)
        advance(lambda p: jnp.concatenate(conv(1, p, p, pl.ds(base, step)), axis=1), base, step)

    def last_window():
        advance(lambda p: pend[p], cols, LAG)

    def state_out():
        return pltpu.make_async_copy(state.at[:, inner], out_next, osem.at[0])

    if not fused:
        lax.fori_loop(0, chunks, lambda j, c: (window(j), c)[1], 0)
        last_window()
        state_out().start()
        state_out().wait()
        finish_halo(xt, 0)
        finish_halo(hid, 1)
        return

    width = cols // members
    ratio = width // step

    def owned(owner):
        start = owner * width + LAG
        if not isinstance(start, int):
            start = pl.multiple_of(start, LAG)
        return pl.ds(start, width)

    def state_copy(owner, sender):
        return pltpu.make_async_remote_copy(
            src_ref=state.at[:, owned(owner)],
            dst_ref=ens_in.at[sender],
            send_sem=es.at[owner],
            recv_sem=er.at[sender],
            device_id={"member": owner},
            device_id_type=MESH,
        )

    def back_copy(owner, member):
        return pltpu.make_async_remote_copy(
            src_ref=back_out,
            dst_ref=back_in.at[owner],
            send_sem=bs.at[member],
            recv_sem=br.at[owner],
            device_id={"member": member},
            device_id_type=MESH,
        )

    def ensemble():
        for d in range(1, members):
            other = lax.rem(me_m + d, members)
            state_copy(me_m, other).wait_recv()
        for o in range(outs):
            sub = pl.ds(o * rows, rows)
            one = jnp.zeros((rows, width), F32)
            two = jnp.zeros((rows, width), F32)
            for m in range(members):
                value = ens_in[m, sub, :]
                one = one + value
                two = two + value * value
            mean = one / members
            var = two / members - mean * mean
            factor = jnp.sqrt(1.0 + target[o] / (var + 1.0))
            back_out[0, sub, :] = regr[sub, :] + (mean - mean * factor)
            back_out[1, sub, :] = factor
        for d in range(1, members):
            back_copy(me_m, lax.rem(me_m + d, members)).start()
        mine = pl.ds(pl.multiple_of(me_m * width, width), width)
        field[:, mine] = back_out[0] + state[:, owned(me_m)] * back_out[1]

    def hand_over(owner):
        @pl.when(owner != me_m)
        def _():
            state_copy(owner, me_m).start()

        @pl.when(owner == me_m)
        def _():
            ens_in[me_m] = state[:, owned(owner)]

    def turn_of(j, carry):
        window(j)

        @pl.when((j >= ratio) & (j % ratio == 0))
        def _():
            hand_over(j // ratio - 1)

        @pl.when(j == (me_m + 1) * ratio + 1)
        def _():
            ensemble()

        return carry

    lax.fori_loop(0, chunks, turn_of, 0)
    last_window()
    hand_over(members - 1)

    @pl.when((me_m + 1) * ratio + 1 >= chunks)
    def _():
        ensemble()

    state_out().start()

    def collect(d, carry):
        owner = lax.rem(me_m + d, members)
        back_copy(owner, owner).wait_recv()
        at = pl.ds(pl.multiple_of(owner * width, width), width)
        field[:, at] = back_in[owner, 0] + state[:, owned(owner)] * back_in[owner, 1]
        return carry

    lax.fori_loop(1, members, collect, 0)
    field_out = pltpu.make_async_copy(field, out_field, osem.at[1])
    field_out.start()
    for d in range(1, members):
        other = lax.rem(me_m + d, members)
        state_copy(other, me_m).wait_send()
        back_copy(me_m, other).wait_send()
    finish_halo(xt, 0)
    finish_halo(hid, 1)
    state_out().wait()
    field_out.wait()


def shards(
    features,
    residual_state,
    noise,
    regression_mean,
    step_index,
    conv_first,
    conv_second,
    head_weight,
    spread_target,
):
    tiles = lax.axis_size("tile")
    members = lax.axis_size("member")
    _, chans, rows, cols = features.shape
    outs = residual_state.shape[1]
    step = 256
    fused = (cols // members) % step == 0
    flat = outs * rows
    padded = rows + 2
    vmem = pl.BlockSpec(memory_space=pltpu.VMEM)
    smem = pl.BlockSpec(memory_space=pltpu.SMEM)
    anywhere = pl.BlockSpec(memory_space=pl.ANY)
    operands = [
        (smem, step_index),
        (smem, spread_target),
        (anywhere, features.reshape(chans * rows, cols)),
        (anywhere, residual_state.reshape(flat, cols)),
        (anywhere, noise.reshape(flat, cols)),
        (anywhere, regression_mean.reshape(flat, cols // members)),
        (anywhere, conv_first),
        (anywhere, conv_second),
        (vmem, head_weight),
    ]
    if not fused:
        del operands[5]
    dma = pltpu.SemaphoreType.DMA
    scratch = [pltpu.VMEM((2 * chans, cols), BF16) for _ in range(rows // 2 + 1)] + [
        pltpu.VMEM((chans * rows, cols), BF16),
        pltpu.VMEM((padded * chans, LAG + cols), BF16),
        pltpu.VMEM((padded * chans, LAG + cols), BF16),
        pltpu.VMEM((2, 6 * chans, 4 * chans), BF16),
        pltpu.VMEM((rows // 2, flat, 2 * chans), BF16),
        pltpu.VMEM((256, 256), BF16),
        pltpu.VMEM((chans, 128), F32),
        pltpu.VMEM((chans, 128), F32),
        pltpu.VMEM((chans, 128), F32),
        pltpu.VMEM((chans, 128), F32),
        pltpu.VMEM((chans, 128), F32),
        pltpu.VMEM((2, tiles, 8, chans), F32),
        pltpu.VMEM((flat, LAG + cols), F32),
        pltpu.VMEM((flat, LAG + cols), F32),
        pltpu.VMEM(conv_first.shape, BF16),
        pltpu.VMEM(conv_second.shape, BF16),
        pltpu.VMEM((rows // 2, 2 * chans, LAG), F32),
        pltpu.VMEM((rows // 2, 2 * chans, LAG), F32),
        pltpu.VMEM((flat, LAG + cols), F32),
        dma((chans * rows // 256,)),
        dma((2, tiles)),
        dma((2, tiles)),
        dma((2, 2)),
        dma((2, 2)),
        dma((5,)),
    ]
    if fused:
        scratch += [
            pltpu.VMEM((members, flat, cols // members), F32),
            pltpu.VMEM((2, flat, cols // members), F32),
            pltpu.VMEM((members, 2, flat, cols // members), F32),
            pltpu.VMEM((flat, cols // members), F32),
            pltpu.VMEM((flat, cols), F32),
            dma((members,)),
            dma((members,)),
            dma((members,)),
            dma((members,)),
        ]
    result = pl.pallas_call(
        functools.partial(kernel, tiles, members, fused, chans, rows, cols, step),
        out_shape=[jax.ShapeDtypeStruct((flat, cols), F32)] * (2 if fused else 1),
        in_specs=[spec for spec, _ in operands],
        out_specs=[anywhere] * (2 if fused else 1),
        scratch_shapes=scratch,
        compiler_params=pltpu.CompilerParams(
            collective_id=0, has_side_effects=True, vmem_limit_bytes=62 * 1024 * 1024
        ),
    )(*[value for _, value in operands])
    advanced = result[0].reshape(outs, rows, cols)
    if fused:
        return (result[1].reshape(1, outs, rows, cols), advanced[None])
    target = spread_target[:, None, None]
    regional = lax.all_gather(regression_mean, "member", axis=2, tiled=True)
    first, second = lax.psum((advanced, advanced * advanced), "member")
    ens_mean = first / members
    ens_var = second / members - ens_mean * ens_mean
    factor = jnp.sqrt(1.0 + target / (ens_var + 1.0))
    field = regional + ens_mean + (advanced - ens_mean) * factor
    return (field[None], advanced[None])


def solution(mesh):
    return jax.shard_map(
        shards,
        mesh=mesh,
        in_specs=(
            P("member", None, "tile", None),
            P("member", None, "tile", None),
            P("member", None, "tile", None),
            P(None, "tile", "member"),
            P(),
            P(),
            P(),
            P(),
            P(),
        ),
        out_specs=(P("member", None, "tile", None), P("member", None, "tile", None)),
        check_vma=False,
    )
```

```python
import functools

import jax
import jax.numpy as jnp
from jax import lax
from jax.experimental import pallas as pl
from jax.experimental.pallas import tpu as pltpu
from jax.sharding import PartitionSpec as P

GROUPS = 32
EPS = 1e-05
F32 = jnp.float32
BF16 = jnp.bfloat16
MESH = pl.DeviceIdType.MESH
LAG = 128


def log2(n):
    assert n & (n - 1) == 0
    return n.bit_length() - 1


def lane_to_row(column):
    n = column.shape[0]
    same = lax.broadcasted_iota(jnp.int32, (n, n), 0) == lax.broadcasted_iota(jnp.int32, (n, n), 1)
    return jnp.sum(jnp.where(same, column, 0.0), axis=0, keepdims=True)


def kernel(tiles, members, fused, chans, rows, cols, step, *refs):
    if fused:
        (coef, target, feat, resid_h, noise_h, regr_h, wa_h, wb_h, head, out_next, out_field) = refs[:11]
        refs = refs[11:]
    else:
        (coef, target, feat, resid_h, noise_h, wa_h, wb_h, head, out_next) = refs[:9]
        refs = refs[9:]
    acts = refs[: rows // 2 + 1]
    refs = refs[rows // 2 + 1 :]
    (fbuf, xt, hid, wide, hw, perm, pivot, acc1, acc2, meanb, rstdb, stat, resid, noise, wa, wb,
     pend, carry_m, state, fsem, ssem, rsem, hs, hr, osem) = refs[:25]
    if fused:
        ens_in, ens_out, back_out, back_in, gain_out, gain_in, regr, field, es, er, bs, br, gs, gr = refs[25:]
    me_t = lax.axis_index("tile")
    me_m = lax.axis_index("member")
    top = me_t > 0
    bottom = me_t < tiles - 1
    chunks = cols // step
    per = 256 // rows
    parts = chans // per
    pairs = rows // 2

    for k in range(parts):
        pltpu.make_async_copy(
            feat.at[pl.ds(k * 256, 256)], fbuf.at[pl.ds(k * 256, 256)], fsem.at[k]
        ).start()
    inner = pl.ds(LAG, cols)
    pairs_of = [(wa_h, wa), (wb_h, wb), (resid_h, resid.at[:, inner]), (noise_h, noise.at[:, inner])]
    if fused:
        pairs_of.append((regr_h, regr))
    loads = [pltpu.make_async_copy(a, b, osem.at[n]) for n, (a, b) in enumerate(pairs_of)]
    for load in loads:
        load.start()

    barrier = pltpu.get_barrier_semaphore()
    for d in range(1, tiles):
        pl.semaphore_signal(barrier, inc=1, device_id={"tile": lax.rem(me_t + d, tiles)}, device_id_type=MESH)
    greet = tiles - 1
    if fused:
        for d in range(1, members):
            pl.semaphore_signal(
                barrier, inc=1, device_id={"member": lax.rem(me_m + d, members)}, device_id_type=MESH
            )
        greet += members - 1

    hw[...] = jnp.zeros_like(hw)
    outs = head.shape[0]
    head32 = head[...].astype(F32)
    for p in range(pairs):
        for out_row in range(2):
            place = lax.broadcasted_iota(jnp.int32, (rows, chans), 0) == 2 * p + out_row
            for o in range(outs):
                hw[p, o * rows : (o + 1) * rows, out_row * chans : (out_row + 1) * chans] = jnp.where(
                    place, head32[o : o + 1, :], 0.0
                ).astype(BF16)
    to = lax.broadcasted_iota(jnp.int32, (256, 256), 0)
    frm = lax.broadcasted_iota(jnp.int32, (256, 256), 1)
    perm[...] = jnp.where((to & (per - 1)) * rows + (to >> log2(per)) == frm, 1.0, 0.0).astype(BF16)
    acc1[...] = jnp.zeros_like(acc1)
    acc2[...] = jnp.zeros_like(acc2)

    def fold(values):
        total = values[:, :128]
        for at in range(128, values.shape[1], 128):
            total = total + values[:, at : at + 128]
        return total

    def set_pivot(start, block):
        size = block.shape[0]
        pivot[pl.ds(start, size), :] = jnp.broadcast_to(
            jnp.mean(block[:, :128], axis=1, keepdims=True), (size, 128)
        )

    def accumulate(start, blocks):
        size = blocks[0].shape[0]
        where = pl.ds(start, size)
        base = pivot[where, :]
        one = jnp.zeros((size, 128), F32)
        two = jnp.zeros((size, 128), F32)
        for block in blocks:
            for at in range(0, block.shape[1], 128):
                off = block[:, at : at + 128] - base
                one = one + off
                two = two + off * off
        acc1[where, :] += one
        acc2[where, :] += two

    for k in range(parts):
        pltpu.make_async_copy(
            feat.at[pl.ds(k * 256, 256)], fbuf.at[pl.ds(k * 256, 256)], fsem.at[k]
        ).wait()

        def spread(j, carry, k=k):
            at = pl.ds(pl.multiple_of(j * step, step), step)
            moved = jnp.dot(perm[...], fbuf[k * 256 : (k + 1) * 256, at], preferred_element_type=F32)
            blocks = [moved[r * per : (r + 1) * per] for r in range(rows)]
            for r in range(rows):
                start = (1 + r) * chans + k * per
                xt[start : start + per, pl.ds(pl.multiple_of(j * step + LAG, LAG), step)] = blocks[r].astype(BF16)
            accumulate(k * per, blocks)
            return carry

        ahead = jnp.dot(
            perm[...], fbuf[k * 256 : (k + 1) * 256, 0:128], preferred_element_type=F32
        )
        set_pivot(k * per, ahead[:per])
        lax.fori_loop(0, chunks, spread, 0, unroll=4)

    pl.semaphore_wait(barrier, greet)

    def halo(buf, turn, side):
        mine, theirs = ((1, rows + 1), (rows, 0))[side]
        return pltpu.make_async_remote_copy(
            src_ref=buf.at[pl.ds(mine * chans, chans), pl.ds(LAG, cols)],
            dst_ref=buf.at[pl.ds(theirs * chans, chans), pl.ds(LAG, cols)],
            send_sem=hs.at[turn, side],
            recv_sem=hr.at[turn, side],
            device_id={"tile": me_t - 1 if side == 0 else me_t + 1},
            device_id_type=MESH,
        )

    def send_halo(buf, turn, side):
        @pl.when(top if side == 0 else bottom)
        def _():
            halo(buf, turn, side).start()

    def stat_copy(turn, src, dev, d):
        return pltpu.make_async_remote_copy(
            src_ref=stat.at[turn, src],
            dst_ref=stat.at[turn, src],
            send_sem=ssem.at[turn, d],
            recv_sem=rsem.at[turn, src],
            device_id={"tile": dev},
            device_id_type=MESH,
        )

    def fill_weights():
        wide[...] = jnp.zeros_like(wide)
        loads[0].wait()
        loads[1].wait()
        for which, source in enumerate((wa, wb)):
            for out_row in range(2):
                for tap_row in range(3):
                    for tap_col in range(3):
                        at = (out_row + tap_row) * chans
                        to_row = (2 * tap_col + out_row) * chans
                        wide[which, to_row : to_row + chans, at : at + chans] = source[
                            3 * tap_row + tap_col
                        ]

    count = rows * cols

    def norm_values(turn, meanwhile):
        one = jnp.sum(acc1[...], axis=1, keepdims=True)
        two = jnp.sum(acc2[...], axis=1, keepdims=True)
        mean = pivot[:, 0:1] + one / count
        dev2 = jnp.maximum(two - one * one / count, 0.0)
        row_id = lax.broadcasted_iota(jnp.int32, (8, chans), 0)
        stat[turn, me_t] = jnp.where(row_id == 0, lane_to_row(mean), lane_to_row(dev2))
        for d in range(1, tiles):
            stat_copy(turn, me_t, lax.rem(me_t + d, tiles), d).start()
        meanwhile()
        for d in range(1, tiles):
            other = lax.rem(me_t + d, tiles)
            stat_copy(turn, other, other, d).wait_recv()
        size = chans // GROUPS
        group = (
            lax.broadcasted_iota(jnp.int32, (chans, chans), 0) >> log2(size)
            == lax.broadcasted_iota(jnp.int32, (chans, chans), 1) >> log2(size)
        )
        every = [stat[turn, t] for t in range(tiles)]
        total = sum(one_of[0:1, :] for one_of in every)
        gmean = jnp.sum(jnp.where(group, total, 0.0), axis=1, keepdims=True) / (size * tiles)
        dev = jnp.zeros((chans, chans), F32)
        for one_of in every:
            gap = one_of[0:1, :] - gmean
            dev = dev + (one_of[1:2, :] + count * (gap * gap))
        gvar = jnp.sum(jnp.where(group, dev, 0.0), axis=1, keepdims=True) / (size * tiles * count)
        meanb[...] = jnp.broadcast_to(gmean, meanb.shape)
        rstdb[...] = jnp.broadcast_to(0.5 * lax.rsqrt(gvar + EPS), rstdb.shape)
        for d in range(1, tiles):
            stat_copy(turn, me_t, lax.rem(me_t + d, tiles), d).wait_send()

    blocks_of = chans // 16

    def activate_block(src, row, block):
        here = pl.ds(pl.multiple_of(block * 16, 16), 16)
        value = src[pl.ds(pl.multiple_of(row * chans + block * 16, 16), 16), LAG:].astype(F32)
        half = (value - meanb[here, 0:1]) * rstdb[here, 0:1]
        start = pl.multiple_of((row % 2) * chans + block * 16, 16)
        acts[row // 2][pl.ds(start, 16), :] = (half + half * jnp.tanh(half)).astype(BF16)

    def activate(src, row):
        def body(block, carry):
            activate_block(src, row, block)
            return carry

        lax.fori_loop(0, blocks_of, body, 0, unroll=4)

    def activate_edge(buf, turn, row):
        side, there = (1, top) if row == 0 else (0, bottom)

        @pl.when(there)
        def _():
            halo(buf, turn, side).wait_recv()
            activate(buf, row)

        @pl.when(jnp.logical_not(there))
        def _():
            start = (row % 2) * chans
            acts[row // 2][start : start + chans, :] = jnp.zeros((chans, cols), BF16)

    def finish_halo(buf, turn):
        for side, there in ((0, top), (1, bottom)):
            @pl.when(there)
            def _(side=side):
                halo(buf, turn, side).wait_send()

    lane = lax.broadcasted_iota(jnp.int32, (2 * chans, LAG), 1)

    def conv(which, p, slot, at):
        taps = jnp.dot(
            wide[which],
            jnp.concatenate([acts[p][:, at], acts[p + 1][:, at]], axis=0),
            preferred_element_type=F32,
        )
        left, centre, right = (taps[n * 2 * chans : (n + 1) * 2 * chans] for n in range(3))
        left0, left1 = (pltpu.roll(left[:, n : n + LAG], 1, 1) for n in (0, LAG))
        right0, right1 = (pltpu.roll(right[:, n : n + LAG], LAG - 1, 1) for n in (0, LAG))
        before = pend[slot] + jnp.where(lane == LAG - 1, right0, 0.0)
        first = (
            centre[:, :LAG]
            + jnp.where(lane == 0, carry_m[slot], left0)
            + jnp.where(lane == LAG - 1, right1, right0)
        )
        pend[slot] = (
            centre[:, LAG:]
            + jnp.where(lane == 0, left0, left1)
            + jnp.where(lane == LAG - 1, 0.0, right1)
        )
        carry_m[slot] = left1
        return before, first

    send_halo(xt, 0, 0)
    send_halo(xt, 0, 1)
    norm_values(0, fill_weights)
    acc1[...] = jnp.zeros_like(acc1)
    acc2[...] = jnp.zeros_like(acc2)

    def first_conv(p, first, beside):
        each = blocks_of // chunks
        rows_at = slice((1 + 2 * p) * chans, (3 + 2 * p) * chans)
        pend[0] = jnp.zeros_like(pend[0])
        carry_m[0] = jnp.zeros_like(carry_m[0])

        def keep(blocks, starts, pivot_now):
            kept = []
            for block, start in zip(blocks, starts):
                rounded = block.astype(BF16)
                hid[rows_at, pl.ds(start, LAG)] = rounded
                wide_block = rounded.astype(F32)
                kept += [wide_block[:chans], wide_block[chans:]]
            if pivot_now:
                set_pivot(0, kept[0])
            accumulate(0, kept)

        def over_cols(j, carry):
            base = j * step
            if not isinstance(j, int):
                base = pl.multiple_of(base, step)
            blocks = conv(0, p, 0, pl.ds(base, step))
            for row in beside:
                for n in range(each):
                    activate_block(xt, row, j * each + n)
            if isinstance(j, int) and j == 0:
                keep(blocks[1:], [LAG], first)
            else:
                keep(blocks, [base, base + LAG if isinstance(j, int) else pl.multiple_of(base + LAG, LAG)], False)
            return carry

        def two_chunks(n, carry):
            return over_cols(2 * n + 1, over_cols(2 * n, carry))

        over_cols(1, over_cols(0, 0))
        lax.fori_loop(1, chunks // 2, two_chunks, 0)
        keep([pend[0]], [cols], False)

    for row in (1, 2, 3):
        activate(xt, row)
    activate_edge(xt, 0, 0)
    first_conv(0, True, [rows - 2, rows - 1, rows])
    send_halo(hid, 1, 0)
    activate_edge(xt, 0, rows + 1)
    middle = list(range(4, rows - 2))
    first_conv(pairs - 1, False, middle)
    send_halo(hid, 1, 1)
    for p in range(1, pairs - 1):
        first_conv(p, False, [])
    norm_values(1, lambda: None)
    for row in range(1, rows + 1):
        activate(hid, row)
    activate_edge(hid, 1, 0)
    activate_edge(hid, 1, rows + 1)
    for load in loads[2:]:
        load.wait()

    at_step = jnp.full((8, 128), coef[0], jnp.int32).astype(F32)
    upper = 800.0 ** (1.0 / 7.0)
    lower = 0.002 ** (1.0 / 7.0)

    def level(place):
        base = upper + place / 17.0 * (lower - upper)
        square = base * base
        return base * square * (square * square)

    sigma = level(at_step)
    sigma_next = level(at_step + 1.0)
    sigma_hat = 1.25 * sigma
    spread_of = jnp.sqrt(sigma_hat * sigma_hat - sigma * sigma)[0:1, 0:1]
    c_skip = (0.25 / (sigma_hat * sigma_hat + 0.25))[0:1, 0:1]
    c_out = (0.5 * sigma_hat / jnp.sqrt(sigma_hat * sigma_hat + 0.25))[0:1, 0:1]
    drift = ((sigma_next - sigma_hat) / sigma_hat)[0:1, 0:1]

    def advance(blocks_of_pair, start, size):
        at = pl.ds(start, size)
        network = jnp.zeros((outs * rows, size), F32)
        for p in range(pairs):
            first_row = (1 + 2 * p) * chans
            block = (xt[first_row : first_row + 2 * chans, at].astype(F32) + blocks_of_pair(p)).astype(BF16)
            network = network + jnp.dot(hw[p], block, preferred_element_type=F32)
        state_hat = resid[:, at] + spread_of * noise[:, at]
        denoised = c_skip * state_hat + c_out * network
        state[:, at] = state_hat + drift * (state_hat - denoised)

    pend[...] = jnp.zeros_like(pend)
    carry_m[...] = jnp.zeros_like(carry_m)

    def window(j):
        base = pl.multiple_of(j * step, step)
        advance(lambda p: jnp.concatenate(conv(1, p, p, pl.ds(base, step)), axis=1), base, step)

    def last_window():
        advance(lambda p: pend[p], cols, LAG)

    def state_out():
        return pltpu.make_async_copy(state.at[:, inner], out_next, osem.at[0])

    if not fused:
        lax.fori_loop(0, chunks, lambda j, c: (window(j), c)[1], 0)
        last_window()
        state_out().start()
        state_out().wait()
        finish_halo(xt, 0)
        finish_halo(hid, 1)
        return

    width = cols // members
    ratio = width // step

    def owned(owner):
        start = owner * width + LAG
        if not isinstance(start, int):
            start = pl.multiple_of(start, LAG)
        return pl.ds(start, width)

    def state_copy(owner, sender):
        return pltpu.make_async_remote_copy(
            src_ref=ens_out.at[owner],
            dst_ref=ens_in.at[sender],
            send_sem=es.at[owner],
            recv_sem=er.at[sender],
            device_id={"member": owner},
            device_id_type=MESH,
        )

    def back_copy(owner, member):
        return pltpu.make_async_remote_copy(
            src_ref=back_out,
            dst_ref=back_in.at[owner],
            send_sem=bs.at[member],
            recv_sem=br.at[owner],
            device_id={"member": member},
            device_id_type=MESH,
        )

    def gain_copy(owner, member):
        return pltpu.make_async_remote_copy(
            src_ref=gain_out,
            dst_ref=gain_in.at[owner],
            send_sem=gs.at[member],
            recv_sem=gr.at[owner],
            device_id={"member": member},
            device_id_type=MESH,
        )

    def ensemble():
        for d in range(1, members):
            other = lax.rem(me_m + d, members)
            state_copy(me_m, other).wait_recv()
        values = [ens_in[m].astype(F32) for m in range(members)]
        gains = []
        for o in range(outs):
            sub = pl.ds(o * rows, rows)
            one = jnp.zeros((rows, width), F32)
            two = jnp.zeros((rows, width), F32)
            for m in range(members):
                value = values[m][o * rows : (o + 1) * rows]
                one = one + value
                two = two + value * value
            mean = one / members
            var = two / members - mean * mean
            factor = jnp.sqrt(1.0 + target[o] / (var + 1.0))
            back_out[sub, :] = regr[sub, :] + (mean - mean * factor)
            gains.append(factor - 1.0)
        gain = jnp.concatenate(gains, axis=0)
        gain_out[...] = gain.astype(BF16)
        for d in range(1, members):
            back_copy(me_m, lax.rem(me_m + d, members)).start()
            gain_copy(me_m, lax.rem(me_m + d, members)).start()
        mine = pl.ds(pl.multiple_of(me_m * width, width), width)
        own = state[:, owned(me_m)]
        field[:, mine] = back_out[...] + (own + own * gain)

    def hand_over(owner):
        @pl.when(owner != me_m)
        def _():
            ens_out[owner] = state[:, owned(owner)].astype(BF16)
            state_copy(owner, me_m).start()

        @pl.when(owner == me_m)
        def _():
            ens_in[me_m] = state[:, owned(owner)].astype(BF16)

    def turn_of(j, carry):
        window(j)

        @pl.when((j >= ratio) & (j % ratio == 0))
        def _():
            hand_over(j // ratio - 1)

        @pl.when(j == (me_m + 1) * ratio + 1)
        def _():
            ensemble()

        return carry

    lax.fori_loop(0, chunks, turn_of, 0)
    last_window()
    hand_over(members - 1)

    @pl.when((me_m + 1) * ratio + 1 >= chunks)
    def _():
        ensemble()

    state_out().start()

    def collect(owner, carry):
        @pl.when(owner != me_m)
        def _():
            back_copy(owner, owner).wait_recv()
            gain_copy(owner, owner).wait_recv()
            at = pl.ds(pl.multiple_of(owner * width, width), width)
            own = state[:, owned(owner)]
            field[:, at] = back_in[owner] + (own + own * gain_in[owner].astype(F32))

        return carry

    lax.fori_loop(0, members, collect, 0)
    field_out = pltpu.make_async_copy(field, out_field, osem.at[1])
    field_out.start()
    for d in range(1, members):
        other = lax.rem(me_m + d, members)
        state_copy(other, me_m).wait_send()
        back_copy(me_m, other).wait_send()
        gain_copy(me_m, other).wait_send()
    finish_halo(xt, 0)
    finish_halo(hid, 1)
    state_out().wait()
    field_out.wait()


def shards(
    features,
    residual_state,
    noise,
    regression_mean,
    step_index,
    conv_first,
    conv_second,
    head_weight,
    spread_target,
):
    tiles = lax.axis_size("tile")
    members = lax.axis_size("member")
    _, chans, rows, cols = features.shape
    outs = residual_state.shape[1]
    step = 256
    fused = (cols // members) % step == 0
    flat = outs * rows
    padded = rows + 2
    vmem = pl.BlockSpec(memory_space=pltpu.VMEM)
    smem = pl.BlockSpec(memory_space=pltpu.SMEM)
    anywhere = pl.BlockSpec(memory_space=pl.ANY)
    operands = [
        (smem, step_index),
        (smem, spread_target),
        (anywhere, features.reshape(chans * rows, cols)),
        (anywhere, residual_state.reshape(flat, cols)),
        (anywhere, noise.reshape(flat, cols)),
        (anywhere, regression_mean.reshape(flat, cols // members)),
        (anywhere, conv_first),
        (anywhere, conv_second),
        (vmem, head_weight),
    ]
    if not fused:
        del operands[5]
    dma = pltpu.SemaphoreType.DMA
    scratch = [pltpu.VMEM((2 * chans, cols), BF16) for _ in range(rows // 2 + 1)] + [
        pltpu.VMEM((chans * rows, cols), BF16),
        pltpu.VMEM((padded * chans, LAG + cols), BF16),
        pltpu.VMEM((padded * chans, LAG + cols), BF16),
        pltpu.VMEM((2, 6 * chans, 4 * chans), BF16),
        pltpu.VMEM((rows // 2, flat, 2 * chans), BF16),
        pltpu.VMEM((256, 256), BF16),
        pltpu.VMEM((chans, 128), F32),
        pltpu.VMEM((chans, 128), F32),
        pltpu.VMEM((chans, 128), F32),
        pltpu.VMEM((chans, 128), F32),
        pltpu.VMEM((chans, 128), F32),
        pltpu.VMEM((2, tiles, 8, chans), F32),
        pltpu.VMEM((flat, LAG + cols), F32),
        pltpu.VMEM((flat, LAG + cols), F32),
        pltpu.VMEM(conv_first.shape, BF16),
        pltpu.VMEM(conv_second.shape, BF16),
        pltpu.VMEM((rows // 2, 2 * chans, LAG), F32),
        pltpu.VMEM((rows // 2, 2 * chans, LAG), F32),
        pltpu.VMEM((flat, LAG + cols), F32),
        dma((chans * rows // 256,)),
        dma((2, tiles)),
        dma((2, tiles)),
        dma((2, 2)),
        dma((2, 2)),
        dma((5,)),
    ]
    if fused:
        scratch += [
            pltpu.VMEM((members, flat, cols // members), BF16),
            pltpu.VMEM((members, flat, cols // members), BF16),
            pltpu.VMEM((flat, cols // members), F32),
            pltpu.VMEM((members, flat, cols // members), F32),
            pltpu.VMEM((flat, cols // members), BF16),
            pltpu.VMEM((members, flat, cols // members), BF16),
            pltpu.VMEM((flat, cols // members), F32),
            pltpu.VMEM((flat, cols), F32),
            dma((members,)),
            dma((members,)),
            dma((members,)),
            dma((members,)),
            dma((members,)),
            dma((members,)),
        ]
    result = pl.pallas_call(
        functools.partial(kernel, tiles, members, fused, chans, rows, cols, step),
        out_shape=[jax.ShapeDtypeStruct((flat, cols), F32)] * (2 if fused else 1),
        in_specs=[spec for spec, _ in operands],
        out_specs=[anywhere] * (2 if fused else 1),
        scratch_shapes=scratch,
        compiler_params=pltpu.CompilerParams(
            collective_id=0, has_side_effects=True, vmem_limit_bytes=62 * 1024 * 1024
        ),
    )(*[value for _, value in operands])
    advanced = result[0].reshape(outs, rows, cols)
    if fused:
        return (result[1].reshape(1, outs, rows, cols), advanced[None])
    target = spread_target[:, None, None]
    regional = lax.all_gather(regression_mean, "member", axis=2, tiled=True)
    first, second = lax.psum((advanced, advanced * advanced), "member")
    ens_mean = first / members
    ens_var = second / members - ens_mean * ens_mean
    factor = jnp.sqrt(1.0 + target / (ens_var + 1.0))
    field = regional + ens_mean + (advanced - ens_mean) * factor
    return (field[None], advanced[None])


def solution(mesh):
    return jax.shard_map(
        shards,
        mesh=mesh,
        in_specs=(
            P("member", None, "tile", None),
            P("member", None, "tile", None),
            P("member", None, "tile", None),
            P(None, "tile", "member"),
            P(),
            P(),
            P(),
            P(),
            P(),
        ),
        out_specs=(P("member", None, "tile", None), P("member", None, "tile", None)),
        check_vma=False,
    )
```

```python
import functools

import jax
import jax.numpy as jnp
from jax import lax
from jax.experimental import pallas as pl
from jax.experimental.pallas import tpu as pltpu
from jax.sharding import PartitionSpec as P

GROUPS = 32
EPS = 1e-05
F32 = jnp.float32
BF16 = jnp.bfloat16
MESH = pl.DeviceIdType.MESH
LAG = 128


def log2(n):
    assert n & (n - 1) == 0
    return n.bit_length() - 1


def lane_to_row(column):
    n = column.shape[0]
    same = lax.broadcasted_iota(jnp.int32, (n, n), 0) == lax.broadcasted_iota(jnp.int32, (n, n), 1)
    return jnp.sum(jnp.where(same, column, 0.0), axis=0, keepdims=True)


def kernel(tiles, members, fused, chans, rows, cols, step, *refs):
    if fused:
        (coef, target, feat, resid_h, noise_h, regr_h, wa_h, wb_h, head, out_next, out_field) = refs[:11]
        refs = refs[11:]
    else:
        (coef, target, feat, resid_h, noise_h, wa_h, wb_h, head, out_next) = refs[:9]
        refs = refs[9:]
    acts = refs[: rows // 2 + 1]
    refs = refs[rows // 2 + 1 :]
    (fbuf, xt, hid, wide, hw, perm, pivot, acc1, acc2, meanb, rstdb, stat, resid, noise, wa, wb,
     pend, carry_m, state, fsem, ssem, rsem, hs, hr, osem) = refs[:25]
    if fused:
        ens_in, ens_out, back_out, back_in, gain_out, gain_in, regr, field, es, er, bs, br, gs, gr = refs[25:]
    me_t = lax.axis_index("tile")
    me_m = lax.axis_index("member")
    top = me_t > 0
    bottom = me_t < tiles - 1
    chunks = cols // step
    per = 256 // rows
    parts = chans // per
    pairs = rows // 2

    for k in range(parts):
        pltpu.make_async_copy(
            feat.at[pl.ds(k * 256, 256)], fbuf.at[pl.ds(k * 256, 256)], fsem.at[k]
        ).start()
    inner = pl.ds(LAG, cols)
    pairs_of = [(wa_h, wa), (wb_h, wb), (resid_h, resid.at[:, inner]), (noise_h, noise.at[:, inner])]
    if fused:
        pairs_of.append((regr_h, regr))
    loads = [pltpu.make_async_copy(a, b, osem.at[n]) for n, (a, b) in enumerate(pairs_of)]
    for load in loads:
        load.start()

    barrier = pltpu.get_barrier_semaphore()
    for d in range(1, tiles):
        pl.semaphore_signal(barrier, inc=1, device_id={"tile": lax.rem(me_t + d, tiles)}, device_id_type=MESH)
    greet = tiles - 1
    if fused:
        for d in range(1, members):
            pl.semaphore_signal(
                barrier, inc=1, device_id={"member": lax.rem(me_m + d, members)}, device_id_type=MESH
            )
        greet += members - 1

    hw[...] = jnp.zeros_like(hw)
    outs = head.shape[0]
    head32 = head[...].astype(F32)
    for p in range(pairs):
        for out_row in range(2):
            place = lax.broadcasted_iota(jnp.int32, (rows, chans), 0) == 2 * p + out_row
            for o in range(outs):
                hw[p, o * rows : (o + 1) * rows, out_row * chans : (out_row + 1) * chans] = jnp.where(
                    place, head32[o : o + 1, :], 0.0
                ).astype(BF16)
    to = lax.broadcasted_iota(jnp.int32, (256, 256), 0)
    frm = lax.broadcasted_iota(jnp.int32, (256, 256), 1)
    perm[...] = jnp.where((to & (per - 1)) * rows + (to >> log2(per)) == frm, 1.0, 0.0).astype(BF16)
    acc1[...] = jnp.zeros_like(acc1)
    acc2[...] = jnp.zeros_like(acc2)

    def fold(values):
        total = values[:, :128]
        for at in range(128, values.shape[1], 128):
            total = total + values[:, at : at + 128]
        return total

    def set_pivot(start, block):
        size = block.shape[0]
        pivot[pl.ds(start, size), :] = jnp.broadcast_to(
            jnp.mean(block[:, :128], axis=1, keepdims=True), (size, 128)
        )

    def accumulate(start, blocks):
        size = blocks[0].shape[0]
        where = pl.ds(start, size)
        base = pivot[where, :]
        one = jnp.zeros((size, 128), F32)
        two = jnp.zeros((size, 128), F32)
        for block in blocks:
            for at in range(0, block.shape[1], 128):
                off = block[:, at : at + 128] - base
                one = one + off
                two = two + off * off
        acc1[where, :] += one
        acc2[where, :] += two

    for k in range(parts):
        pltpu.make_async_copy(
            feat.at[pl.ds(k * 256, 256)], fbuf.at[pl.ds(k * 256, 256)], fsem.at[k]
        ).wait()

        def spread(j, carry, k=k):
            at = pl.ds(pl.multiple_of(j * step, step), step)
            moved = jnp.dot(perm[...], fbuf[k * 256 : (k + 1) * 256, at], preferred_element_type=F32)
            blocks = [moved[r * per : (r + 1) * per] for r in range(rows)]
            for r in range(rows):
                start = (1 + r) * chans + k * per
                xt[start : start + per, pl.ds(pl.multiple_of(j * step + LAG, LAG), step)] = blocks[r].astype(BF16)
            accumulate(k * per, blocks)
            return carry

        ahead = jnp.dot(
            perm[...], fbuf[k * 256 : (k + 1) * 256, 0:128], preferred_element_type=F32
        )
        set_pivot(k * per, ahead[:per])
        lax.fori_loop(0, chunks, spread, 0, unroll=4)

    pl.semaphore_wait(barrier, greet)

    def halo(buf, turn, side):
        mine, theirs = ((1, rows + 1), (rows, 0))[side]
        return pltpu.make_async_remote_copy(
            src_ref=buf.at[pl.ds(mine * chans, chans), pl.ds(LAG, cols)],
            dst_ref=buf.at[pl.ds(theirs * chans, chans), pl.ds(LAG, cols)],
            send_sem=hs.at[turn, side],
            recv_sem=hr.at[turn, side],
            device_id={"tile": me_t - 1 if side == 0 else me_t + 1},
            device_id_type=MESH,
        )

    def send_halo(buf, turn, side):
        @pl.when(top if side == 0 else bottom)
        def _():
            halo(buf, turn, side).start()

    def stat_copy(turn, src, dev, d):
        return pltpu.make_async_remote_copy(
            src_ref=stat.at[turn, src],
            dst_ref=stat.at[turn, src],
            send_sem=ssem.at[turn, d],
            recv_sem=rsem.at[turn, src],
            device_id={"tile": dev},
            device_id_type=MESH,
        )

    def fill_weights():
        wide[...] = jnp.zeros_like(wide)
        loads[0].wait()
        loads[1].wait()
        for which, source in enumerate((wa, wb)):
            for out_row in range(2):
                for tap_row in range(3):
                    for tap_col in range(3):
                        at = (out_row + tap_row) * chans
                        to_row = (2 * tap_col + out_row) * chans
                        wide[which, to_row : to_row + chans, at : at + chans] = source[
                            3 * tap_row + tap_col
                        ]

    count = rows * cols

    def norm_values(turn, meanwhile):
        one = jnp.sum(acc1[...], axis=1, keepdims=True)
        two = jnp.sum(acc2[...], axis=1, keepdims=True)
        mean = pivot[:, 0:1] + one / count
        dev2 = jnp.maximum(two - one * one / count, 0.0)
        row_id = lax.broadcasted_iota(jnp.int32, (8, chans), 0)
        stat[turn, me_t] = jnp.where(row_id == 0, lane_to_row(mean), lane_to_row(dev2))
        for d in range(1, tiles):
            stat_copy(turn, me_t, lax.rem(me_t + d, tiles), d).start()
        meanwhile()
        for d in range(1, tiles):
            other = lax.rem(me_t + d, tiles)
            stat_copy(turn, other, other, d).wait_recv()
        size = chans // GROUPS
        group = (
            lax.broadcasted_iota(jnp.int32, (chans, chans), 0) >> log2(size)
            == lax.broadcasted_iota(jnp.int32, (chans, chans), 1) >> log2(size)
        )
        every = [stat[turn, t] for t in range(tiles)]
        total = sum(one_of[0:1, :] for one_of in every)
        gmean = jnp.sum(jnp.where(group, total, 0.0), axis=1, keepdims=True) / (size * tiles)
        dev = jnp.zeros((chans, chans), F32)
        for one_of in every:
            gap = one_of[0:1, :] - gmean
            dev = dev + (one_of[1:2, :] + count * (gap * gap))
        gvar = jnp.sum(jnp.where(group, dev, 0.0), axis=1, keepdims=True) / (size * tiles * count)
        meanb[...] = jnp.broadcast_to(gmean, meanb.shape)
        rstdb[...] = jnp.broadcast_to(0.5 * lax.rsqrt(gvar + EPS), rstdb.shape)
        for d in range(1, tiles):
            stat_copy(turn, me_t, lax.rem(me_t + d, tiles), d).wait_send()

    blocks_of = chans // 16

    def activate_block(src, row, block):
        here = pl.ds(pl.multiple_of(block * 16, 16), 16)
        value = src[pl.ds(pl.multiple_of(row * chans + block * 16, 16), 16), LAG:].astype(F32)
        half = (value - meanb[here, 0:1]) * rstdb[here, 0:1]
        start = pl.multiple_of((row % 2) * chans + block * 16, 16)
        acts[row // 2][pl.ds(start, 16), :] = (half + half * jnp.tanh(half)).astype(BF16)

    def activate(src, row):
        def body(block, carry):
            activate_block(src, row, block)
            return carry

        lax.fori_loop(0, blocks_of, body, 0, unroll=4)

    def activate_edge(buf, turn, row):
        side, there = (1, top) if row == 0 else (0, bottom)

        @pl.when(there)
        def _():
            halo(buf, turn, side).wait_recv()
            activate(buf, row)

        @pl.when(jnp.logical_not(there))
        def _():
            start = (row % 2) * chans
            acts[row // 2][start : start + chans, :] = jnp.zeros((chans, cols), BF16)

    def finish_halo(buf, turn):
        for side, there in ((0, top), (1, bottom)):
            @pl.when(there)
            def _(side=side):
                halo(buf, turn, side).wait_send()

    lane = lax.broadcasted_iota(jnp.int32, (2 * chans, LAG), 1)

    def conv(which, p, slot, at):
        taps = jnp.dot(
            wide[which],
            jnp.concatenate([acts[p][:, at], acts[p + 1][:, at]], axis=0),
            preferred_element_type=F32,
        )
        left, centre, right = (taps[n * 2 * chans : (n + 1) * 2 * chans] for n in range(3))
        left0, left1 = (pltpu.roll(left[:, n : n + LAG], 1, 1) for n in (0, LAG))
        right0, right1 = (pltpu.roll(right[:, n : n + LAG], LAG - 1, 1) for n in (0, LAG))
        before = pend[slot] + jnp.where(lane == LAG - 1, right0, 0.0)
        first = (
            centre[:, :LAG]
            + jnp.where(lane == 0, carry_m[slot], left0)
            + jnp.where(lane == LAG - 1, right1, right0)
        )
        pend[slot] = (
            centre[:, LAG:]
            + jnp.where(lane == 0, left0, left1)
            + jnp.where(lane == LAG - 1, 0.0, right1)
        )
        carry_m[slot] = left1
        return before, first

    send_halo(xt, 0, 0)
    send_halo(xt, 0, 1)
    norm_values(0, fill_weights)
    acc1[...] = jnp.zeros_like(acc1)
    acc2[...] = jnp.zeros_like(acc2)

    def first_conv(p, first, beside):
        each = blocks_of // chunks
        rows_at = slice((1 + 2 * p) * chans, (3 + 2 * p) * chans)
        pend[0] = jnp.zeros_like(pend[0])
        carry_m[0] = jnp.zeros_like(carry_m[0])

        def keep(blocks, starts, pivot_now):
            kept = []
            for block, start in zip(blocks, starts):
                rounded = block.astype(BF16)
                hid[rows_at, pl.ds(start, LAG)] = rounded
                wide_block = rounded.astype(F32)
                kept += [wide_block[:chans], wide_block[chans:]]
            if pivot_now:
                set_pivot(0, kept[0])
            accumulate(0, kept)

        def over_cols(j, carry):
            base = j * step
            if not isinstance(j, int):
                base = pl.multiple_of(base, step)
            blocks = conv(0, p, 0, pl.ds(base, step))
            for row in beside:
                for n in range(each):
                    activate_block(xt, row, j * each + n)
            if isinstance(j, int) and j == 0:
                keep(blocks[1:], [LAG], first)
            else:
                keep(blocks, [base, base + LAG if isinstance(j, int) else pl.multiple_of(base + LAG, LAG)], False)
            return carry

        def two_chunks(n, carry):
            return over_cols(2 * n + 1, over_cols(2 * n, carry))

        over_cols(1, over_cols(0, 0))
        lax.fori_loop(1, chunks // 2, two_chunks, 0)
        keep([pend[0]], [cols], False)

    for row in range(2, rows - 2):
        activate(xt, row)
    first_conv(1, True, [1, rows])
    activate_edge(xt, 0, 0)
    first_conv(0, False, [rows - 2, rows - 1])
    send_halo(hid, 1, 0)
    activate_edge(xt, 0, rows + 1)
    first_conv(pairs - 1, False, [])
    send_halo(hid, 1, 1)
    for p in range(2, pairs - 1):
        first_conv(p, False, [])
    norm_values(1, lambda: None)
    for row in range(1, rows + 1):
        activate(hid, row)
    activate_edge(hid, 1, 0)
    activate_edge(hid, 1, rows + 1)
    for load in loads[2:]:
        load.wait()

    at_step = jnp.full((8, 128), coef[0], jnp.int32).astype(F32)
    upper = 800.0 ** (1.0 / 7.0)
    lower = 0.002 ** (1.0 / 7.0)

    def level(place):
        base = upper + place / 17.0 * (lower - upper)
        square = base * base
        return base * square * (square * square)

    sigma = level(at_step)
    sigma_next = level(at_step + 1.0)
    sigma_hat = 1.25 * sigma
    spread_of = jnp.sqrt(sigma_hat * sigma_hat - sigma * sigma)[0:1, 0:1]
    c_skip = (0.25 / (sigma_hat * sigma_hat + 0.25))[0:1, 0:1]
    c_out = (0.5 * sigma_hat / jnp.sqrt(sigma_hat * sigma_hat + 0.25))[0:1, 0:1]
    drift = ((sigma_next - sigma_hat) / sigma_hat)[0:1, 0:1]

    def advance(blocks_of_pair, start, size):
        at = pl.ds(start, size)
        network = jnp.zeros((outs * rows, size), F32)
        for p in range(pairs):
            first_row = (1 + 2 * p) * chans
            block = (xt[first_row : first_row + 2 * chans, at].astype(F32) + blocks_of_pair(p)).astype(BF16)
            network = network + jnp.dot(hw[p], block, preferred_element_type=F32)
        state_hat = resid[:, at] + spread_of * noise[:, at]
        denoised = c_skip * state_hat + c_out * network
        state[:, at] = state_hat + drift * (state_hat - denoised)

    pend[...] = jnp.zeros_like(pend)
    carry_m[...] = jnp.zeros_like(carry_m)

    def window(j):
        base = pl.multiple_of(j * step, step)
        advance(lambda p: jnp.concatenate(conv(1, p, p, pl.ds(base, step)), axis=1), base, step)

    def last_window():
        advance(lambda p: pend[p], cols, LAG)

    def state_out():
        return pltpu.make_async_copy(state.at[:, inner], out_next, osem.at[0])

    if not fused:
        lax.fori_loop(0, chunks, lambda j, c: (window(j), c)[1], 0)
        last_window()
        state_out().start()
        state_out().wait()
        finish_halo(xt, 0)
        finish_halo(hid, 1)
        return

    width = cols // members
    ratio = width // step

    def owned(owner):
        start = owner * width + LAG
        if not isinstance(start, int):
            start = pl.multiple_of(start, LAG)
        return pl.ds(start, width)

    def state_copy(owner, sender):
        return pltpu.make_async_remote_copy(
            src_ref=ens_out.at[owner],
            dst_ref=ens_in.at[sender],
            send_sem=es.at[owner],
            recv_sem=er.at[sender],
            device_id={"member": owner},
            device_id_type=MESH,
        )

    def back_copy(owner, member):
        return pltpu.make_async_remote_copy(
            src_ref=back_out,
            dst_ref=back_in.at[owner],
            send_sem=bs.at[member],
            recv_sem=br.at[owner],
            device_id={"member": member},
            device_id_type=MESH,
        )

    def gain_copy(owner, member):
        return pltpu.make_async_remote_copy(
            src_ref=gain_out,
            dst_ref=gain_in.at[owner],
            send_sem=gs.at[member],
            recv_sem=gr.at[owner],
            device_id={"member": member},
            device_id_type=MESH,
        )

    def ensemble():
        for d in range(1, members):
            other = lax.rem(me_m + d, members)
            state_copy(me_m, other).wait_recv()
        values = [ens_in[m].astype(F32) for m in range(members)]
        gains = []
        for o in range(outs):
            sub = pl.ds(o * rows, rows)
            one = jnp.zeros((rows, width), F32)
            two = jnp.zeros((rows, width), F32)
            for m in range(members):
                value = values[m][o * rows : (o + 1) * rows]
                one = one + value
                two = two + value * value
            mean = one / members
            var = two / members - mean * mean
            factor = jnp.sqrt(1.0 + target[o] / (var + 1.0))
            back_out[sub, :] = regr[sub, :] + (mean - mean * factor)
            gains.append(factor - 1.0)
        gain = jnp.concatenate(gains, axis=0)
        gain_out[...] = gain.astype(BF16)
        for d in range(1, members):
            back_copy(me_m, lax.rem(me_m + d, members)).start()
            gain_copy(me_m, lax.rem(me_m + d, members)).start()
        mine = pl.ds(pl.multiple_of(me_m * width, width), width)
        own = state[:, owned(me_m)]
        field[:, mine] = back_out[...] + (own + own * gain)

    def hand_over(owner):
        @pl.when(owner != me_m)
        def _():
            ens_out[owner] = state[:, owned(owner)].astype(BF16)
            state_copy(owner, me_m).start()

        @pl.when(owner == me_m)
        def _():
            ens_in[me_m] = state[:, owned(owner)].astype(BF16)

    def turn_of(j, carry):
        window(j)

        @pl.when((j >= ratio) & (j % ratio == 0))
        def _():
            hand_over(j // ratio - 1)

        @pl.when(j == (me_m + 1) * ratio + 1)
        def _():
            ensemble()

        return carry

    lax.fori_loop(0, chunks, turn_of, 0)
    last_window()
    hand_over(members - 1)

    @pl.when((me_m + 1) * ratio + 1 >= chunks)
    def _():
        ensemble()

    state_out().start()

    def collect(owner, carry):
        @pl.when(owner != me_m)
        def _():
            back_copy(owner, owner).wait_recv()
            gain_copy(owner, owner).wait_recv()
            at = pl.ds(pl.multiple_of(owner * width, width), width)
            own = state[:, owned(owner)]
            field[:, at] = back_in[owner] + (own + own * gain_in[owner].astype(F32))

        return carry

    lax.fori_loop(0, members, collect, 0)
    field_out = pltpu.make_async_copy(field, out_field, osem.at[1])
    field_out.start()
    for d in range(1, members):
        other = lax.rem(me_m + d, members)
        state_copy(other, me_m).wait_send()
        back_copy(me_m, other).wait_send()
        gain_copy(me_m, other).wait_send()
    finish_halo(xt, 0)
    finish_halo(hid, 1)
    state_out().wait()
    field_out.wait()


def shards(
    features,
    residual_state,
    noise,
    regression_mean,
    step_index,
    conv_first,
    conv_second,
    head_weight,
    spread_target,
):
    tiles = lax.axis_size("tile")
    members = lax.axis_size("member")
    _, chans, rows, cols = features.shape
    outs = residual_state.shape[1]
    step = 256
    fused = (cols // members) % step == 0
    flat = outs * rows
    padded = rows + 2
    vmem = pl.BlockSpec(memory_space=pltpu.VMEM)
    smem = pl.BlockSpec(memory_space=pltpu.SMEM)
    anywhere = pl.BlockSpec(memory_space=pl.ANY)
    operands = [
        (smem, step_index),
        (smem, spread_target),
        (anywhere, features.reshape(chans * rows, cols)),
        (anywhere, residual_state.reshape(flat, cols)),
        (anywhere, noise.reshape(flat, cols)),
        (anywhere, regression_mean.reshape(flat, cols // members)),
        (anywhere, conv_first),
        (anywhere, conv_second),
        (vmem, head_weight),
    ]
    if not fused:
        del operands[5]
    dma = pltpu.SemaphoreType.DMA
    scratch = [pltpu.VMEM((2 * chans, cols), BF16) for _ in range(rows // 2 + 1)] + [
        pltpu.VMEM((chans * rows, cols), BF16),
        pltpu.VMEM((padded * chans, LAG + cols), BF16),
        pltpu.VMEM((padded * chans, LAG + cols), BF16),
        pltpu.VMEM((2, 6 * chans, 4 * chans), BF16),
        pltpu.VMEM((rows // 2, flat, 2 * chans), BF16),
        pltpu.VMEM((256, 256), BF16),
        pltpu.VMEM((chans, 128), F32),
        pltpu.VMEM((chans, 128), F32),
        pltpu.VMEM((chans, 128), F32),
        pltpu.VMEM((chans, 128), F32),
        pltpu.VMEM((chans, 128), F32),
        pltpu.VMEM((2, tiles, 8, chans), F32),
        pltpu.VMEM((flat, LAG + cols), F32),
        pltpu.VMEM((flat, LAG + cols), F32),
        pltpu.VMEM(conv_first.shape, BF16),
        pltpu.VMEM(conv_second.shape, BF16),
        pltpu.VMEM((rows // 2, 2 * chans, LAG), F32),
        pltpu.VMEM((rows // 2, 2 * chans, LAG), F32),
        pltpu.VMEM((flat, LAG + cols), F32),
        dma((chans * rows // 256,)),
        dma((2, tiles)),
        dma((2, tiles)),
        dma((2, 2)),
        dma((2, 2)),
        dma((5,)),
    ]
    if fused:
        scratch += [
            pltpu.VMEM((members, flat, cols // members), BF16),
            pltpu.VMEM((members, flat, cols // members), BF16),
            pltpu.VMEM((flat, cols // members), F32),
            pltpu.VMEM((members, flat, cols // members), F32),
            pltpu.VMEM((flat, cols // members), BF16),
            pltpu.VMEM((members, flat, cols // members), BF16),
            pltpu.VMEM((flat, cols // members), F32),
            pltpu.VMEM((flat, cols), F32),
            dma((members,)),
            dma((members,)),
            dma((members,)),
            dma((members,)),
            dma((members,)),
            dma((members,)),
        ]
    result = pl.pallas_call(
        functools.partial(kernel, tiles, members, fused, chans, rows, cols, step),
        out_shape=[jax.ShapeDtypeStruct((flat, cols), F32)] * (2 if fused else 1),
        in_specs=[spec for spec, _ in operands],
        out_specs=[anywhere] * (2 if fused else 1),
        scratch_shapes=scratch,
        compiler_params=pltpu.CompilerParams(
            collective_id=0, has_side_effects=True, vmem_limit_bytes=62 * 1024 * 1024
        ),
    )(*[value for _, value in operands])
    advanced = result[0].reshape(outs, rows, cols)
    if fused:
        return (result[1].reshape(1, outs, rows, cols), advanced[None])
    target = spread_target[:, None, None]
    regional = lax.all_gather(regression_mean, "member", axis=2, tiled=True)
    first, second = lax.psum((advanced, advanced * advanced), "member")
    ens_mean = first / members
    ens_var = second / members - ens_mean * ens_mean
    factor = jnp.sqrt(1.0 + target / (ens_var + 1.0))
    field = regional + ens_mean + (advanced - ens_mean) * factor
    return (field[None], advanced[None])


def solution(mesh):
    return jax.shard_map(
        shards,
        mesh=mesh,
        in_specs=(
            P("member", None, "tile", None),
            P("member", None, "tile", None),
            P("member", None, "tile", None),
            P(None, "tile", "member"),
            P(),
            P(),
            P(),
            P(),
            P(),
        ),
        out_specs=(P("member", None, "tile", None), P("member", None, "tile", None)),
        check_vma=False,
    )
```

```python
import functools

import jax
import jax.numpy as jnp
from jax import lax
from jax.experimental import pallas as pl
from jax.experimental.pallas import tpu as pltpu
from jax.sharding import PartitionSpec as P

GROUPS = 32
EPS = 1e-05
F32 = jnp.float32
BF16 = jnp.bfloat16
MESH = pl.DeviceIdType.MESH
LAG = 128


def log2(n):
    assert n & (n - 1) == 0
    return n.bit_length() - 1


def lane_to_row(column):
    n = column.shape[0]
    same = lax.broadcasted_iota(jnp.int32, (n, n), 0) == lax.broadcasted_iota(jnp.int32, (n, n), 1)
    return jnp.sum(jnp.where(same, column, 0.0), axis=0, keepdims=True)


def kernel(tiles, members, fused, chans, rows, cols, step, *refs):
    if fused:
        (coef, target, feat, resid_h, noise_h, regr_h, wa_h, wb_h, head, out_next, out_field) = refs[:11]
        refs = refs[11:]
    else:
        (coef, target, feat, resid_h, noise_h, wa_h, wb_h, head, out_next) = refs[:9]
        refs = refs[9:]
    acts = refs[: rows // 2 + 1]
    refs = refs[rows // 2 + 1 :]
    (fbuf, xt, hid, wide, hw, perm, pivot, acc1, acc2, meanb, rstdb, stat, resid, noise, wa, wb,
     pend, carry_m, state, fsem, ssem, rsem, hs, hr, osem) = refs[:25]
    if fused:
        ens_in, ens_out, back_out, back_in, gain_out, gain_in, regr, field, es, er, bs, br, gs, gr = refs[25:]
    me_t = lax.axis_index("tile")
    me_m = lax.axis_index("member")
    top = me_t > 0
    bottom = me_t < tiles - 1
    chunks = cols // step
    per = 256 // rows
    parts = chans // per
    pairs = rows // 2

    for k in range(parts):
        pltpu.make_async_copy(
            feat.at[pl.ds(k * 256, 256)], fbuf.at[pl.ds(k * 256, 256)], fsem.at[k]
        ).start()
    inner = pl.ds(LAG, cols)
    pairs_of = [(wa_h, wa), (wb_h, wb), (resid_h, resid.at[:, inner]), (noise_h, noise.at[:, inner])]
    if fused:
        pairs_of.append((regr_h, regr))
    loads = [pltpu.make_async_copy(a, b, osem.at[n]) for n, (a, b) in enumerate(pairs_of)]
    for load in loads:
        load.start()

    barrier = pltpu.get_barrier_semaphore()
    for d in range(1, tiles):
        pl.semaphore_signal(barrier, inc=1, device_id={"tile": lax.rem(me_t + d, tiles)}, device_id_type=MESH)
    greet = tiles - 1
    if fused:
        for d in range(1, members):
            pl.semaphore_signal(
                barrier, inc=1, device_id={"member": lax.rem(me_m + d, members)}, device_id_type=MESH
            )
        greet += members - 1

    hw[...] = jnp.zeros_like(hw)
    outs = head.shape[0]
    head32 = head[...].astype(F32)
    for p in range(pairs):
        for out_row in range(2):
            place = lax.broadcasted_iota(jnp.int32, (rows, chans), 0) == 2 * p + out_row
            for o in range(outs):
                hw[p, o * rows : (o + 1) * rows, out_row * chans : (out_row + 1) * chans] = jnp.where(
                    place, head32[o : o + 1, :], 0.0
                ).astype(BF16)
    to = lax.broadcasted_iota(jnp.int32, (256, 256), 0)
    frm = lax.broadcasted_iota(jnp.int32, (256, 256), 1)
    perm[...] = jnp.where((to & (per - 1)) * rows + (to >> log2(per)) == frm, 1.0, 0.0).astype(BF16)
    acc1[...] = jnp.zeros_like(acc1)
    acc2[...] = jnp.zeros_like(acc2)

    def fold(values):
        total = values[:, :128]
        for at in range(128, values.shape[1], 128):
            total = total + values[:, at : at + 128]
        return total

    def set_pivot(start, block):
        size = block.shape[0]
        pivot[pl.ds(start, size), :] = jnp.broadcast_to(
            jnp.mean(block[:, :128], axis=1, keepdims=True), (size, 128)
        )

    def accumulate(start, blocks):
        size = blocks[0].shape[0]
        where = pl.ds(start, size)
        base = pivot[where, :]
        one = jnp.zeros((size, 128), F32)
        two = jnp.zeros((size, 128), F32)
        for block in blocks:
            for at in range(0, block.shape[1], 128):
                off = block[:, at : at + 128] - base
                one = one + off
                two = two + off * off
        acc1[where, :] += one
        acc2[where, :] += two

    for k in range(parts):
        pltpu.make_async_copy(
            feat.at[pl.ds(k * 256, 256)], fbuf.at[pl.ds(k * 256, 256)], fsem.at[k]
        ).wait()

        def spread(j, carry, k=k):
            at = pl.ds(pl.multiple_of(j * step, step), step)
            moved = jnp.dot(perm[...], fbuf[k * 256 : (k + 1) * 256, at], preferred_element_type=F32)
            blocks = [moved[r * per : (r + 1) * per] for r in range(rows)]
            for r in range(rows):
                start = (1 + r) * chans + k * per
                xt[start : start + per, pl.ds(pl.multiple_of(j * step + LAG, LAG), step)] = blocks[r].astype(BF16)
            accumulate(k * per, blocks)
            return carry

        ahead = jnp.dot(
            perm[...], fbuf[k * 256 : (k + 1) * 256, 0:128], preferred_element_type=F32
        )
        set_pivot(k * per, ahead[:per])
        lax.fori_loop(0, chunks, spread, 0, unroll=8)

    pl.semaphore_wait(barrier, greet)

    def halo(buf, turn, side):
        mine, theirs = ((1, rows + 1), (rows, 0))[side]
        return pltpu.make_async_remote_copy(
            src_ref=buf.at[pl.ds(mine * chans, chans), pl.ds(LAG, cols)],
            dst_ref=buf.at[pl.ds(theirs * chans, chans), pl.ds(LAG, cols)],
            send_sem=hs.at[turn, side],
            recv_sem=hr.at[turn, side],
            device_id={"tile": me_t - 1 if side == 0 else me_t + 1},
            device_id_type=MESH,
        )

    def send_halo(buf, turn, side):
        @pl.when(top if side == 0 else bottom)
        def _():
            halo(buf, turn, side).start()

    def stat_copy(turn, src, dev, d):
        return pltpu.make_async_remote_copy(
            src_ref=stat.at[turn, src],
            dst_ref=stat.at[turn, src],
            send_sem=ssem.at[turn, d],
            recv_sem=rsem.at[turn, src],
            device_id={"tile": dev},
            device_id_type=MESH,
        )

    def fill_weights():
        wide[...] = jnp.zeros_like(wide)
        loads[0].wait()
        loads[1].wait()
        for which, source in enumerate((wa, wb)):
            for out_row in range(2):
                for tap_row in range(3):
                    for tap_col in range(3):
                        at = (out_row + tap_row) * chans
                        to_row = (2 * tap_col + out_row) * chans
                        wide[which, to_row : to_row + chans, at : at + chans] = source[
                            3 * tap_row + tap_col
                        ]

    count = rows * cols

    def norm_values(turn, meanwhile):
        one = jnp.sum(acc1[...], axis=1, keepdims=True)
        two = jnp.sum(acc2[...], axis=1, keepdims=True)
        mean = pivot[:, 0:1] + one / count
        dev2 = jnp.maximum(two - one * one / count, 0.0)
        row_id = lax.broadcasted_iota(jnp.int32, (8, chans), 0)
        stat[turn, me_t] = jnp.where(row_id == 0, lane_to_row(mean), lane_to_row(dev2))
        for d in range(1, tiles):
            stat_copy(turn, me_t, lax.rem(me_t + d, tiles), d).start()
        meanwhile()
        for d in range(1, tiles):
            other = lax.rem(me_t + d, tiles)
            stat_copy(turn, other, other, d).wait_recv()
        size = chans // GROUPS
        group = (
            lax.broadcasted_iota(jnp.int32, (chans, chans), 0) >> log2(size)
            == lax.broadcasted_iota(jnp.int32, (chans, chans), 1) >> log2(size)
        )
        every = [stat[turn, t] for t in range(tiles)]
        total = sum(one_of[0:1, :] for one_of in every)
        gmean = jnp.sum(jnp.where(group, total, 0.0), axis=1, keepdims=True) / (size * tiles)
        dev = jnp.zeros((chans, chans), F32)
        for one_of in every:
            gap = one_of[0:1, :] - gmean
            dev = dev + (one_of[1:2, :] + count * (gap * gap))
        gvar = jnp.sum(jnp.where(group, dev, 0.0), axis=1, keepdims=True) / (size * tiles * count)
        meanb[...] = jnp.broadcast_to(gmean, meanb.shape)
        rstdb[...] = jnp.broadcast_to(0.5 * lax.rsqrt(gvar + EPS), rstdb.shape)
        for d in range(1, tiles):
            stat_copy(turn, me_t, lax.rem(me_t + d, tiles), d).wait_send()

    blocks_of = chans // 16

    def activate_block(src, row, block):
        here = pl.ds(pl.multiple_of(block * 16, 16), 16)
        value = src[pl.ds(pl.multiple_of(row * chans + block * 16, 16), 16), LAG:].astype(F32)
        half = (value - meanb[here, 0:1]) * rstdb[here, 0:1]
        start = pl.multiple_of((row % 2) * chans + block * 16, 16)
        acts[row // 2][pl.ds(start, 16), :] = (half + half * jnp.tanh(half)).astype(BF16)

    def activate(src, row):
        def body(block, carry):
            activate_block(src, row, block)
            return carry

        lax.fori_loop(0, blocks_of, body, 0, unroll=8)

    def activate_edge(buf, turn, row):
        side, there = (1, top) if row == 0 else (0, bottom)

        @pl.when(there)
        def _():
            halo(buf, turn, side).wait_recv()
            activate(buf, row)

        @pl.when(jnp.logical_not(there))
        def _():
            start = (row % 2) * chans
            acts[row // 2][start : start + chans, :] = jnp.zeros((chans, cols), BF16)

    def finish_halo(buf, turn):
        for side, there in ((0, top), (1, bottom)):
            @pl.when(there)
            def _(side=side):
                halo(buf, turn, side).wait_send()

    lane = lax.broadcasted_iota(jnp.int32, (2 * chans, LAG), 1)

    def conv(which, p, slot, at):
        taps = jnp.dot(
            wide[which],
            jnp.concatenate([acts[p][:, at], acts[p + 1][:, at]], axis=0),
            preferred_element_type=F32,
        )
        left, centre, right = (taps[n * 2 * chans : (n + 1) * 2 * chans] for n in range(3))
        left0, left1 = (pltpu.roll(left[:, n : n + LAG], 1, 1) for n in (0, LAG))
        right0, right1 = (pltpu.roll(right[:, n : n + LAG], LAG - 1, 1) for n in (0, LAG))
        before = pend[slot] + jnp.where(lane == LAG - 1, right0, 0.0)
        first = (
            centre[:, :LAG]
            + jnp.where(lane == 0, carry_m[slot], left0)
            + jnp.where(lane == LAG - 1, right1, right0)
        )
        pend[slot] = (
            centre[:, LAG:]
            + jnp.where(lane == 0, left0, left1)
            + jnp.where(lane == LAG - 1, 0.0, right1)
        )
        carry_m[slot] = left1
        return before, first

    send_halo(xt, 0, 0)
    send_halo(xt, 0, 1)
    norm_values(0, fill_weights)
    acc1[...] = jnp.zeros_like(acc1)
    acc2[...] = jnp.zeros_like(acc2)

    def first_conv(p, first, beside):
        each = blocks_of // chunks
        rows_at = slice((1 + 2 * p) * chans, (3 + 2 * p) * chans)
        pend[0] = jnp.zeros_like(pend[0])
        carry_m[0] = jnp.zeros_like(carry_m[0])

        def keep(blocks, starts, pivot_now):
            kept = []
            for block, start in zip(blocks, starts):
                rounded = block.astype(BF16)
                hid[rows_at, pl.ds(start, LAG)] = rounded
                wide_block = rounded.astype(F32)
                kept += [wide_block[:chans], wide_block[chans:]]
            if pivot_now:
                set_pivot(0, kept[0])
            accumulate(0, kept)

        def over_cols(j, carry):
            base = j * step
            if not isinstance(j, int):
                base = pl.multiple_of(base, step)
            blocks = conv(0, p, 0, pl.ds(base, step))
            for row in beside:
                for n in range(each):
                    activate_block(xt, row, j * each + n)
            if isinstance(j, int) and j == 0:
                keep(blocks[1:], [LAG], first)
            else:
                keep(blocks, [base, base + LAG if isinstance(j, int) else pl.multiple_of(base + LAG, LAG)], False)
            return carry

        def two_chunks(n, carry):
            return over_cols(2 * n + 1, over_cols(2 * n, carry))

        over_cols(1, over_cols(0, 0))
        lax.fori_loop(1, chunks // 2, two_chunks, 0)
        keep([pend[0]], [cols], False)

    for row in (1, 2, 3):
        activate(xt, row)
    activate_edge(xt, 0, 0)
    first_conv(0, True, [rows - 2, rows - 1, rows])
    send_halo(hid, 1, 0)
    activate_edge(xt, 0, rows + 1)
    middle = list(range(4, rows - 2))
    first_conv(pairs - 1, False, middle)
    send_halo(hid, 1, 1)
    for p in range(1, pairs - 1):
        first_conv(p, False, [])
    norm_values(1, lambda: None)
    for row in range(1, rows + 1):
        activate(hid, row)
    activate_edge(hid, 1, 0)
    activate_edge(hid, 1, rows + 1)
    for load in loads[2:]:
        load.wait()

    at_step = jnp.full((8, 128), coef[0], jnp.int32).astype(F32)
    upper = 800.0 ** (1.0 / 7.0)
    lower = 0.002 ** (1.0 / 7.0)

    def level(place):
        base = upper + place / 17.0 * (lower - upper)
        square = base * base
        return base * square * (square * square)

    sigma = level(at_step)
    sigma_next = level(at_step + 1.0)
    sigma_hat = 1.25 * sigma
    spread_of = jnp.sqrt(sigma_hat * sigma_hat - sigma * sigma)[0:1, 0:1]
    c_skip = (0.25 / (sigma_hat * sigma_hat + 0.25))[0:1, 0:1]
    c_out = (0.5 * sigma_hat / jnp.sqrt(sigma_hat * sigma_hat + 0.25))[0:1, 0:1]
    drift = ((sigma_next - sigma_hat) / sigma_hat)[0:1, 0:1]

    def advance(blocks_of_pair, start, size):
        at = pl.ds(start, size)
        network = jnp.zeros((outs * rows, size), F32)
        for p in range(pairs):
            first_row = (1 + 2 * p) * chans
            block = (xt[first_row : first_row + 2 * chans, at].astype(F32) + blocks_of_pair(p)).astype(BF16)
            network = network + jnp.dot(hw[p], block, preferred_element_type=F32)
        state_hat = resid[:, at] + spread_of * noise[:, at]
        denoised = c_skip * state_hat + c_out * network
        state[:, at] = state_hat + drift * (state_hat - denoised)

    pend[...] = jnp.zeros_like(pend)
    carry_m[...] = jnp.zeros_like(carry_m)

    def window(j):
        base = pl.multiple_of(j * step, step)
        advance(lambda p: jnp.concatenate(conv(1, p, p, pl.ds(base, step)), axis=1), base, step)

    def last_window():
        advance(lambda p: pend[p], cols, LAG)

    def state_out():
        return pltpu.make_async_copy(state.at[:, inner], out_next, osem.at[0])

    if not fused:
        lax.fori_loop(0, chunks, lambda j, c: (window(j), c)[1], 0)
        last_window()
        state_out().start()
        state_out().wait()
        finish_halo(xt, 0)
        finish_halo(hid, 1)
        return

    width = cols // members
    ratio = width // step

    def owned(owner):
        start = owner * width + LAG
        if not isinstance(start, int):
            start = pl.multiple_of(start, LAG)
        return pl.ds(start, width)

    def state_copy(owner, sender):
        return pltpu.make_async_remote_copy(
            src_ref=ens_out.at[owner],
            dst_ref=ens_in.at[sender],
            send_sem=es.at[owner],
            recv_sem=er.at[sender],
            device_id={"member": owner},
            device_id_type=MESH,
        )

    def back_copy(owner, member):
        return pltpu.make_async_remote_copy(
            src_ref=back_out,
            dst_ref=back_in.at[owner],
            send_sem=bs.at[member],
            recv_sem=br.at[owner],
            device_id={"member": member},
            device_id_type=MESH,
        )

    def gain_copy(owner, member):
        return pltpu.make_async_remote_copy(
            src_ref=gain_out,
            dst_ref=gain_in.at[owner],
            send_sem=gs.at[member],
            recv_sem=gr.at[owner],
            device_id={"member": member},
            device_id_type=MESH,
        )

    def ensemble():
        for d in range(1, members):
            other = lax.rem(me_m + d, members)
            state_copy(me_m, other).wait_recv()
        values = [ens_in[m].astype(F32) for m in range(members)]
        gains = []
        for o in range(outs):
            sub = pl.ds(o * rows, rows)
            one = jnp.zeros((rows, width), F32)
            two = jnp.zeros((rows, width), F32)
            for m in range(members):
                value = values[m][o * rows : (o + 1) * rows]
                one = one + value
                two = two + value * value
            mean = one / members
            var = two / members - mean * mean
            factor = jnp.sqrt(1.0 + target[o] / (var + 1.0))
            back_out[sub, :] = regr[sub, :] + (mean - mean * factor)
            gains.append(factor - 1.0)
        gain = jnp.concatenate(gains, axis=0)
        gain_out[...] = gain.astype(BF16)
        for d in range(1, members):
            back_copy(me_m, lax.rem(me_m + d, members)).start()
            gain_copy(me_m, lax.rem(me_m + d, members)).start()
        mine = pl.ds(pl.multiple_of(me_m * width, width), width)
        own = state[:, owned(me_m)]
        field[:, mine] = back_out[...] + (own + own * gain)

    def hand_over(owner):
        @pl.when(owner != me_m)
        def _():
            ens_out[owner] = state[:, owned(owner)].astype(BF16)
            state_copy(owner, me_m).start()

        @pl.when(owner == me_m)
        def _():
            ens_in[me_m] = state[:, owned(owner)].astype(BF16)

    def turn_of(j, carry):
        window(j)

        @pl.when((j >= ratio) & (j % ratio == 0))
        def _():
            hand_over(j // ratio - 1)

        @pl.when(j == (me_m + 1) * ratio + 1)
        def _():
            ensemble()

        return carry

    lax.fori_loop(0, chunks, turn_of, 0)
    last_window()
    hand_over(members - 1)

    @pl.when((me_m + 1) * ratio + 1 >= chunks)
    def _():
        ensemble()

    state_out().start()

    def collect(owner, carry):
        @pl.when(owner != me_m)
        def _():
            back_copy(owner, owner).wait_recv()
            gain_copy(owner, owner).wait_recv()
            at = pl.ds(pl.multiple_of(owner * width, width), width)
            own = state[:, owned(owner)]
            field[:, at] = back_in[owner] + (own + own * gain_in[owner].astype(F32))

        return carry

    lax.fori_loop(0, members, collect, 0)
    field_out = pltpu.make_async_copy(field, out_field, osem.at[1])
    field_out.start()
    for d in range(1, members):
        other = lax.rem(me_m + d, members)
        state_copy(other, me_m).wait_send()
        back_copy(me_m, other).wait_send()
        gain_copy(me_m, other).wait_send()
    finish_halo(xt, 0)
    finish_halo(hid, 1)
    state_out().wait()
    field_out.wait()


def shards(
    features,
    residual_state,
    noise,
    regression_mean,
    step_index,
    conv_first,
    conv_second,
    head_weight,
    spread_target,
):
    tiles = lax.axis_size("tile")
    members = lax.axis_size("member")
    _, chans, rows, cols = features.shape
    outs = residual_state.shape[1]
    step = 256
    fused = (cols // members) % step == 0
    flat = outs * rows
    padded = rows + 2
    vmem = pl.BlockSpec(memory_space=pltpu.VMEM)
    smem = pl.BlockSpec(memory_space=pltpu.SMEM)
    anywhere = pl.BlockSpec(memory_space=pl.ANY)
    operands = [
        (smem, step_index),
        (smem, spread_target),
        (anywhere, features.reshape(chans * rows, cols)),
        (anywhere, residual_state.reshape(flat, cols)),
        (anywhere, noise.reshape(flat, cols)),
        (anywhere, regression_mean.reshape(flat, cols // members)),
        (anywhere, conv_first),
        (anywhere, conv_second),
        (vmem, head_weight),
    ]
    if not fused:
        del operands[5]
    dma = pltpu.SemaphoreType.DMA
    scratch = [pltpu.VMEM((2 * chans, cols), BF16) for _ in range(rows // 2 + 1)] + [
        pltpu.VMEM((chans * rows, cols), BF16),
        pltpu.VMEM((padded * chans, LAG + cols), BF16),
        pltpu.VMEM((padded * chans, LAG + cols), BF16),
        pltpu.VMEM((2, 6 * chans, 4 * chans), BF16),
        pltpu.VMEM((rows // 2, flat, 2 * chans), BF16),
        pltpu.VMEM((256, 256), BF16),
        pltpu.VMEM((chans, 128), F32),
        pltpu.VMEM((chans, 128), F32),
        pltpu.VMEM((chans, 128), F32),
        pltpu.VMEM((chans, 128), F32),
        pltpu.VMEM((chans, 128), F32),
        pltpu.VMEM((2, tiles, 8, chans), F32),
        pltpu.VMEM((flat, LAG + cols), F32),
        pltpu.VMEM((flat, LAG + cols), F32),
        pltpu.VMEM(conv_first.shape, BF16),
        pltpu.VMEM(conv_second.shape, BF16),
        pltpu.VMEM((rows // 2, 2 * chans, LAG), F32),
        pltpu.VMEM((rows // 2, 2 * chans, LAG), F32),
        pltpu.VMEM((flat, LAG + cols), F32),
        dma((chans * rows // 256,)),
        dma((2, tiles)),
        dma((2, tiles)),
        dma((2, 2)),
        dma((2, 2)),
        dma((5,)),
    ]
    if fused:
        scratch += [
            pltpu.VMEM((members, flat, cols // members), BF16),
            pltpu.VMEM((members, flat, cols // members), BF16),
            pltpu.VMEM((flat, cols // members), F32),
            pltpu.VMEM((members, flat, cols // members), F32),
            pltpu.VMEM((flat, cols // members), BF16),
            pltpu.VMEM((members, flat, cols // members), BF16),
            pltpu.VMEM((flat, cols // members), F32),
            pltpu.VMEM((flat, cols), F32),
            dma((members,)),
            dma((members,)),
            dma((members,)),
            dma((members,)),
            dma((members,)),
            dma((members,)),
        ]
    result = pl.pallas_call(
        functools.partial(kernel, tiles, members, fused, chans, rows, cols, step),
        out_shape=[jax.ShapeDtypeStruct((flat, cols), F32)] * (2 if fused else 1),
        in_specs=[spec for spec, _ in operands],
        out_specs=[anywhere] * (2 if fused else 1),
        scratch_shapes=scratch,
        compiler_params=pltpu.CompilerParams(
            collective_id=0, has_side_effects=True, vmem_limit_bytes=62 * 1024 * 1024
        ),
    )(*[value for _, value in operands])
    advanced = result[0].reshape(outs, rows, cols)
    if fused:
        return (result[1].reshape(1, outs, rows, cols), advanced[None])
    target = spread_target[:, None, None]
    regional = lax.all_gather(regression_mean, "member", axis=2, tiled=True)
    first, second = lax.psum((advanced, advanced * advanced), "member")
    ens_mean = first / members
    ens_var = second / members - ens_mean * ens_mean
    factor = jnp.sqrt(1.0 + target / (ens_var + 1.0))
    field = regional + ens_mean + (advanced - ens_mean) * factor
    return (field[None], advanced[None])


def solution(mesh):
    return jax.shard_map(
        shards,
        mesh=mesh,
        in_specs=(
            P("member", None, "tile", None),
            P("member", None, "tile", None),
            P("member", None, "tile", None),
            P(None, "tile", "member"),
            P(),
            P(),
            P(),
            P(),
            P(),
        ),
        out_specs=(P("member", None, "tile", None), P("member", None, "tile", None)),
        check_vma=False,
    )
```
